32 devices in a mesh: src: 8 (over y, x, core), dst: 4 (over z).
Axes of the slice: x: 2, y: 2, z: 4, core: 2. Of those that a mesh axis runs over, the one named last changes fastest.
Arguments:
- src_table: float32 [400, 8192], P(None, ('src', 'dst')), may hold values from -3 to 3
- src_state: float32 [8192], P(('src', 'dst')), may hold values from 0.01 to 0.1
- dst_table: float32 [400, 8192], P(None, ('src', 'dst')), may hold values from -3 to 3
- dst_state: float32 [8192], P(('src', 'dst')), may hold values from 0.01 to 0.1
- spare_table: float32 [400, 8192], P(None, ('src', 'dst')), may hold values from -3 to 3
- spare_state: float32 [8192], P(('src', 'dst')), may hold values from 0.01 to 0.1
- relations: float32 [400, 16], replicated, may hold values from -1 to 1
- rel_state: float32 [400, 16], replicated, may hold values from 5 to 51
- edge_rows: int32 [2, 2, 8192], P(None, None, ('src', 'dst')), may hold values from 0 to 255
- edge_rel: int32 [2, 8192], P(None, ('src', 'dst')), may hold values from 0 to 15
- counts: int32 [2, 32], P(None, ('src', 'dst')), may hold values from 48 to 256, as said below
- negatives: int32 [2, 16384], P(None, ('src', 'dst')), may hold values from 0 to 255
Outputs:
- src_out: float32 [400, 8192], P(None, ('src', 'dst'))
- src_state_out: float32 [8192], P(('src', 'dst'))
- dst_out: float32 [400, 8192], P(None, ('src', 'dst'))
- dst_state_out: float32 [8192], P(('src', 'dst'))
- spare_out: float32 [400, 8192], P(None, ('src', 'dst'))
- spare_state_out: float32 [8192], P(('src', 'dst'))
- relations_out: float32 [400, 16], replicated
- rel_state_out: float32 [400, 16], replicated
The draws below stay inside these ranges and needn't reach their ends.
Inputs may be any that keep to these rules, and one draw needn't show every extreme that they name: `edge_rows`: local columns of a bucket's source slab (first row) and destination slab (second row). `counts`: in each round some bucket holds exactly 256 valid edges and some exactly 48; edge slots at or past a bucket's count are padding.
All inputs are finite; a program needn't handle non-finite values.
Results may differ from the reference program's by a relative error of at most 0.0003.
Values sent between devices are 32-bit elements; how exact they have to be, the bound alone decides.
No kernel may reach another device: no remote copies, remote signals or barrier semaphores. Data moves between devices by JAX's collectives and lax.ppermute only.
A program may use at most 64 MiB of HBM per device.

```python
import math
import jax
import jax.numpy as jnp
import numpy as np
from jax import lax

D = 400
RELS = 16
NEG = 512
ROWS = 256
EDGES = 256
SLABS = 32
N_SRC = 8
N_DST = 4


def draw_relations(key, part):
    key = jax.random.fold_in(key, 5)
    key_sign, key_size = jax.random.split(key, 2)
    signs = jnp.where(jax.random.uniform(key_sign, (D, RELS)) < 0.5, -1.0, 1.0)
    magnitude = jnp.exp(jax.random.uniform(key_size, (D, RELS), minval=math.log(0.1), maxval=0.0))
    return (signs * magnitude).astype(jnp.float32)


def draw_counts(key, part):
    key = jax.random.fold_in(key, 11)
    key_level, key_jitter, key_full, key_light = jax.random.split(key, 4)
    halving = jax.random.randint(key_level, (2, SLABS), 0, 3)
    levels = jnp.where(halving == 0, EDGES, jnp.where(halving == 1, EDGES // 2, EDGES // 4))
    jitter = jax.random.randint(key_jitter, (2, SLABS), 0, 1000000) % (levels // 4 + 1)
    values = levels - jitter
    fullest = jax.random.randint(key_full, (2, 1), 0, SLABS)
    lightest = (fullest + 1 + jax.random.randint(key_light, (2, 1), 0, SLABS - 1)) % SLABS
    slab_ids = jnp.arange(SLABS, dtype=jnp.int32)[None, :]
    values = jnp.where(slab_ids == fullest, EDGES, values)
    values = jnp.where(slab_ids == lightest, 3 * EDGES // 16, values)
    return values.astype(jnp.int32)


def touch_ends(entries, rng, least, high):
    shape = entries.shape
    place = [jax.random.randint(jax.random.fold_in(rng, axis), (), 0, shape[axis]) for axis in range(len(shape))]
    entries = entries.at[tuple(place)].set(least)
    longest = shape.index(max(shape))
    place[longest] = (place[longest] + 1) % shape[longest]
    return entries.at[tuple(place)].set(high)


def block_scale(key, extent, cuts, smallest, high):
    gain, own = 1.0, jax.random.fold_in(key, 6)
    for position, blocks in cuts:
        steps = jnp.exp(jax.random.uniform(jax.random.fold_in(own, position), (blocks,), jnp.float32, smallest / len(cuts), high / len(cuts)))
        gain = gain * jnp.repeat(steps, extent[position] // blocks).reshape([-1 if axis == position else 1 for axis in range(len(extent))])
    return gain


def rank_table(number_of, slope):
    weights = [(1 << 20) // math.isqrt(standing ** slope) + 1 for standing in range(1, number_of + 1)]
    deviation = 1 + sum(weights) // (1 << 30)
    return np.cumsum(np.array([max(1, weight // deviation) for weight in weights]))


def skewed_ids(stream_key, extent, number_of, lean):
    table = rank_table(number_of, lean)
    ticket = jax.random.randint(jax.random.fold_in(stream_key, 1), extent, 0, int(table[number_of - 1]))
    standing = jnp.searchsorted(jnp.asarray(table, jnp.int32), ticket, side="right")
    return jax.random.permutation(jax.random.fold_in(stream_key, 2), number_of)[standing].astype(jnp.int32)


def centred(key, shape, scale, limit, cuts=(), kind=jnp.bfloat16):
    entries = jax.random.normal(key, shape, jnp.float32) * scale
    if len(cuts) > 0:
        entries = block_scale(key, shape, cuts, -0.22, 0.18) * entries
    return jnp.clip(entries, min=-limit, max=limit).astype(kind)


def setup_inputs(seed: int = 0) -> dict:
    seeds = jax.random.split(jax.random.key(seed), 13)
    return {
        "src_table": centred(seeds[0], (D, SLABS * ROWS), 0.5, 3.0, ((1, 32),), jnp.float32),
        "src_state": jnp.clip(jnp.exp(math.log(0.1) - 2.3025851 * jax.random.uniform(seeds[1], (SLABS * ROWS,), jnp.float32) ** block_scale(seeds[1], (SLABS * ROWS,), ((0, 32),), -0.2, 0.2)), 0.01, 0.1),
        "dst_table": centred(seeds[2], (D, SLABS * ROWS), 0.5, 3.0, ((1, 32),), jnp.float32),
        "dst_state": jnp.clip(jnp.exp(math.log(0.1) - 2.3025851 * jax.random.uniform(seeds[3], (SLABS * ROWS,), jnp.float32) ** block_scale(seeds[3], (SLABS * ROWS,), ((0, 32),), -0.2, 0.2)), 0.01, 0.1),
        "spare_table": centred(seeds[4], (D, SLABS * ROWS), 0.5, 3.0, ((1, 32),), jnp.float32),
        "spare_state": jnp.clip(jnp.exp(math.log(0.1) - 2.3025851 * jax.random.uniform(seeds[5], (SLABS * ROWS,), jnp.float32) ** block_scale(seeds[5], (SLABS * ROWS,), ((0, 32),), -0.2, 0.2)), 0.01, 0.1),
        "relations": draw_relations(jax.random.fold_in(seeds[12], 71), 0),
        "rel_state": jnp.clip(jnp.exp(jax.random.uniform(seeds[7], (D, RELS), jnp.float32, math.log(5.0), math.log(51.0))), 5.0, 51.0),
        "edge_rows": touch_ends(jax.random.randint(seeds[8], (2, 2, SLABS * EDGES), 0, ROWS), jax.random.fold_in(seeds[8], 1), 0, ROWS - 1).astype(jnp.int32),
        "edge_rel": touch_ends(skewed_ids(seeds[9], (2, SLABS * EDGES), RELS, 2), jax.random.fold_in(seeds[9], 3), 0, RELS - 1).astype(jnp.int32),
        "counts": draw_counts(jax.random.fold_in(seeds[12], 71), 0),
        "negatives": touch_ends(jax.random.randint(seeds[11], (2, SLABS * NEG), 0, ROWS), jax.random.fold_in(seeds[11], 1), 0, ROWS - 1).astype(jnp.int32),
    }


ROW_RATE = 0.25
REL_RATE = 0.5
NEG_WEIGHT = 0.0625
PRECISE = lax.Precision.HIGHEST

def bucket_grads(table_src, table_dst, relations, edge_pairs, rel_ids, live_count, negatives):
    source = edge_pairs[0]
    target = edge_pairs[1]
    edge_total = source.shape[0]
    rel_onehot = (rel_ids[None, :] == jnp.arange(relations.shape[1], dtype=jnp.int32)[:, None]).astype(jnp.float32)
    rel_cols = jnp.dot(relations, rel_onehot, precision=PRECISE)
    src_cols = jnp.take(table_src, source, axis=1)
    query = src_cols * rel_cols
    dst_cols = jnp.take(table_dst, target, axis=1)
    neg_cols = jnp.take(table_dst, negatives, axis=1)
    positive = lax.optimization_barrier(jnp.sum(query * dst_cols, axis=0))
    valid_mask = jnp.arange(edge_total, dtype=jnp.int32) < live_count
    pos_grad = jnp.where(valid_mask, -jax.nn.sigmoid(-positive), jnp.float32(0.0))
    neg_scores = lax.dot_general(query, neg_cols, (((0,), (0,)), ((), ())), precision=PRECISE)
    neg_grad = jnp.where(valid_mask[:, None], NEG_WEIGHT * jax.nn.sigmoid(neg_scores), jnp.float32(0.0))
    back_query = lax.dot_general(neg_cols, neg_grad, (((1,), (1,)), ((), ())), precision=PRECISE)
    query_grad = dst_cols * pos_grad[None, :] + back_query
    src_grad = jnp.zeros_like(table_src).at[:, source].add(query_grad * rel_cols)
    rel_grad = lax.dot_general(query_grad * src_cols, rel_onehot, (((1,), (1,)), ((), ())), precision=PRECISE)
    back_table = jnp.dot(query, neg_grad, precision=PRECISE)
    dst_grad = jnp.zeros_like(table_dst).at[:, target].add(query * pos_grad[None, :]).at[:, negatives].add(back_table)
    return (src_grad, dst_grad, rel_grad)

def row_step(table, state, gradient):
    new_state = state + lax.optimization_barrier(jnp.mean(gradient * gradient, axis=0))
    return (table - ROW_RATE * gradient / jnp.sqrt(new_state)[None, :], new_state)

def reference(src_table, src_state, dst_table, dst_state, spare_table, spare_state, relations, rel_state, edge_rows, edge_rel, counts, negatives):
    slab_count = N_SRC * N_DST

    def split_table(table):
        return table.reshape(D, slab_count, ROWS).transpose(1, 0, 2)

    def join_table(stack):
        return stack.transpose(1, 0, 2).reshape(D, slab_count * ROWS)

    def rotate(stack):
        grouped = stack.reshape((N_SRC, N_DST) + stack.shape[1:])
        return jnp.roll(grouped, 1, axis=0).reshape(stack.shape)

    def partner(stack):
        grouped = stack.reshape((N_SRC, N_DST // 2, 2) + stack.shape[1:])
        return jnp.flip(grouped, axis=2).reshape(stack.shape)
    pair_all = edge_rows.reshape(2, 2, slab_count, EDGES).transpose(0, 2, 1, 3)
    rel_all = edge_rel.reshape(2, slab_count, EDGES)
    neg_all = negatives.reshape(2, slab_count, NEG)

    def one_round(inputs):
        table_a, state_a, table_b, state_b, edge_pairs, rel_ids, live_count, neg_ids = inputs
        grad_a, grad_b, grad_rel = bucket_grads(table_a, table_b, relations, edge_pairs, rel_ids, live_count, neg_ids)
        next_a, acc_a = row_step(table_a, state_a, grad_a)
        next_b, acc_b = row_step(table_b, state_b, grad_b)
        return (next_a, acc_a, next_b, acc_b, grad_rel)
    first_src, first_state, dst_next, dst_acc, first_rel = lax.map(one_round, (split_table(src_table), src_state.reshape(slab_count, ROWS), split_table(dst_table), dst_state.reshape(slab_count, ROWS), pair_all[0], rel_all[0], counts[0], neg_all[0]))
    second_src, second_state, spare_next, spare_acc, second_rel = lax.map(one_round, (rotate(first_src), rotate(first_state), partner(split_table(spare_table)), partner(spare_state.reshape(slab_count, ROWS)), pair_all[1], rel_all[1], counts[1], neg_all[1]))
    rel_total = lax.optimization_barrier(jnp.sum(first_rel, axis=0)) + lax.optimization_barrier(jnp.sum(second_rel, axis=0))
    rel_state_out = rel_state + rel_total * rel_total
    relations_out = relations - REL_RATE * rel_total / jnp.sqrt(rel_state_out)
    return (join_table(second_src), second_state.reshape(-1), join_table(dst_next), dst_acc.reshape(-1), join_table(spare_next), spare_acc.reshape(-1), relations_out, rel_state_out)
```

```python
import jax
import jax.numpy as jnp
from jax import lax
from jax.experimental import pallas as pl
from jax.experimental.pallas import tpu as pltpu
from jax.sharding import PartitionSpec as P

ROW_RATE = 0.25
REL_RATE = 0.5
NEG_WEIGHT = 0.0625
F32 = jnp.float32
BF16 = jnp.bfloat16
NN = (((1,), (0,)), ((), ()))
NT = (((1,), (1,)), ((), ()))
TN = (((0,), (0,)), ((), ()))
VMEM = pl.BlockSpec(memory_space=pltpu.VMEM)
HBM = pl.BlockSpec(memory_space=pltpu.HBM)


def swapped(array, axis, stride):
    return lax.ppermute(array, axis, [(i, i ^ 1 << stride) for i in range(lax.axis_size(axis))])


def passed_along(array, axis, by):
    count = lax.axis_size(axis)
    return lax.ppermute(array, axis, [(i, (i + by) % count) for i in range(count)])


def radices(count):
    steps = []
    while count > 1:
        steps.append(4 if count % 4 == 0 else 2)
        count //= steps[-1]
    return steps


def exchanged_terms(array):
    n_src, n_dst = lax.axis_size("src"), lax.axis_size("dst")
    steps = [("src", 1, 2)]
    for axis, count, stride in (("src", n_src // 2, 2), ("dst", n_dst, 1)):
        for radix in radices(count):
            steps.append((axis, stride, radix))
            stride *= radix
    terms = [array]
    for axis, stride, radix in steps:
        array = tree_sum(terms)
        count = lax.axis_size(axis)
        terms = [array]
        for k in range(1, radix):
            terms.append(lax.ppermute(array, axis, [(i, i ^ k * stride) for i in range(count)]))
    return terms


def tree_sum(terms):
    while len(terms) > 1:
        terms = [a + b for a, b in zip(terms[::2], terms[1::2])]
    return terms[0]


def packed_shape(rels, features):
    whole, rest = divmod(features, 128)
    assert rest * rels <= 8 * 128 and rels % 8 == 0
    return (whole * rels + (8 if rest else 0), 128)


def pack(out, values):
    rels, features = values.shape
    whole, rest = divmod(features, 128)
    for k in range(whole):
        out[k * rels : (k + 1) * rels, :] = values[:, k * 128 : (k + 1) * 128]
    if rest:
        tail = [values[8 * k : 8 * (k + 1), whole * 128 :] for k in range(rels // 8)]
        tail.append(jnp.zeros((8, 128 - rest * len(tail)), F32))
        out[whole * rels :, :] = jnp.concatenate(tail, axis=1)


def unpack(packed, rels, features):
    whole, rest = divmod(features, 128)
    parts = [packed[k * rels : (k + 1) * rels, :] for k in range(whole)]
    if rest:
        tail = packed[whole * rels :, :]
        tails = [tail[:, k * rest : (k + 1) * rest] for k in range(rels // 8)]
        parts.append(jnp.concatenate(tails, axis=0))
    return jnp.concatenate(parts, axis=1)


def halves(x):
    high = x.astype(BF16)
    return high, (x - high.astype(F32)).astype(BF16)


def dot(a, b, dims):
    return lax.dot_general(a, b, dims, preferred_element_type=F32)


def dot_split(a, b, dims):
    return dot(a[0], b[0], dims) + dot(a[0], b[1], dims) + dot(a[1], b[0], dims)


def dot_left(a, b, dims):
    return dot(a[0], b, dims) + dot(a[1], b, dims)


def dot_right(a, b, dims):
    return dot(a, b[0], dims) + dot(a, b[1], dims)


def onehot(index, length):
    return index == lax.broadcasted_iota(jnp.int32, (length, index.shape[1]), 0)


def as_bf16(mask):
    return jnp.where(mask, 1.0, 0.0).astype(BF16)


def negative_weight(negatives, rows, edges):
    ones = jnp.ones((negatives.shape[1], edges), BF16)
    return NEG_WEIGHT * dot(as_bf16(onehot(negatives, rows)), ones, NN)


def coefficients(query, table_rows, weight, at_target, valid):
    scores = dot_split(table_rows, halves(query), NN)
    positive = jnp.sum(jnp.where(at_target, scores, 0.0), axis=0, keepdims=True)
    pos_grad = jnp.where(valid, -1.0 / (1.0 + jnp.exp(positive)), 0.0)
    neg_grad = jnp.where(valid, weight / (1.0 + jnp.exp(-scores)), 0.0)
    return neg_grad + jnp.where(at_target, pos_grad, 0.0)


def row_step(table, state, gradient):
    new_state = state + jnp.sum(gradient * gradient, axis=0, keepdims=True) * (1.0 / table.shape[0])
    return table - gradient * (ROW_RATE / jnp.sqrt(new_state)), new_state


def hot_relations(round_id, edge_rel, rels):
    return as_bf16(onehot(edge_rel[round_id : round_id + 1, :], rels))


def edge_parts(round_id, rows_of_table, rel, edge_rows, edge_rel, counts, negatives):
    edges = edge_rows.shape[2]
    rel_hot = hot_relations(round_id, edge_rel, rel.shape[0])
    src_hot = as_bf16(onehot(edge_rows[round_id, 0:1, :], rows_of_table))
    at_target = onehot(edge_rows[round_id, 1:2, :], rows_of_table)
    rel_cols = dot_left(halves(rel[...]), rel_hot, TN)
    place = lax.broadcasted_iota(jnp.int32, (1, edges), 1)
    valid = place < counts[:, round_id : round_id + 1]
    weight = negative_weight(negatives[round_id : round_id + 1, :], rows_of_table, edges)
    return src_hot, at_target, rel_cols, valid, weight


def first_front_kernel(
    src_hbm, state_hbm, dst_hbm, rel_hbm, rows_hbm, rels_hbm, counts_hbm, negs_hbm,
    moved_out, query_out, coef_out, product_out,
    src, src_state, dst, rel, rows, rels, counts, negs, sems,
):
    pairs = [
        (rows_hbm, rows), (rels_hbm, rels), (rel_hbm, rel), (counts_hbm, counts),
        (negs_hbm, negs), (dst_hbm, dst), (src_hbm, src), (state_hbm, src_state),
    ]
    copies = [pltpu.make_async_copy(a, b, sems.at[i]) for i, (a, b) in enumerate(pairs)]
    for copy in copies:
        copy.start()
    for copy in copies[:5]:
        copy.wait()
    features, columns = src.shape
    src_hot, at_target, rel_cols, valid, weight = edge_parts(
        0, columns, rel, rows, rels, counts, negs
    )
    copies[5].wait()
    table_dst = halves(dst[...])
    table_rows = halves(dst[...].T)
    copies[6].wait()
    src_cols = dot_left(halves(src[...]), src_hot, NN)
    query = src_cols * rel_cols
    coef = coefficients(query, table_rows, weight, at_target, valid)
    query_grad = dot_split(table_dst, halves(coef), NN)
    src_grad = dot_left(halves(query_grad * rel_cols), src_hot, NT)
    copies[7].wait()
    table, state = row_step(src[...], src_state[...], src_grad)
    moved_out[0:features, :] = table
    moved_out[features:, :] = jnp.broadcast_to(state, (moved_out.shape[0] - features, columns))
    query_out[...] = query
    coef_out[...] = coef
    product_out[...] = query_grad * src_cols


def first_back_kernel(
    dst, dst_state, query, coef, product, rel, rows, rels, counts, negs,
    spare_state, table_out, state_out, rel_first_out, rel_cols_out, weight_out, live_out, spare_out,
):
    grad = dot_split(halves(query[...]), halves(coef[...]), NT)
    table_out[...], state_out[...] = row_step(dst[...], dst_state[...], grad)
    edges, columns = rows.shape[2], dst.shape[1]
    rel_first_out[...] = dot_right(
        hot_relations(0, rels, rel.shape[0]), halves(product[...]), NT
    )
    rel_cols_out[...] = dot_left(halves(rel[...]), hot_relations(1, rels, rel.shape[0]), TN)
    weight_out[...] = negative_weight(negs[1:2, :], columns, edges)
    place = lax.broadcasted_iota(jnp.int32, (1, edges), 1)
    live_out[...] = jnp.where(place < counts[:, 1:2], 1.0, 0.0)
    spare_out[...] = spare_state[...]


def spare_kernel(spare, rows_high, rows_low, high, low):
    rows_high[...], rows_low[...] = halves(spare[...].T)
    high[...], low[...] = halves(spare[...])


def second_front_kernel(
    moved, rows_high, rows_low, high, low, rel_cols, weight, live, rows, rels, rel_first,
    state, query_out, coef_out, scaled_out, rel_out, state_out,
):
    features, columns = high.shape
    rel_hot = hot_relations(1, rels, rel_first.shape[0])
    src_hot = as_bf16(onehot(rows[1, 0:1, :], columns))
    at_target = onehot(rows[1, 1:2, :], columns)
    valid = live[...] > 0.0
    src_cols = dot_left(halves(moved[0:features, :]), src_hot, NN)
    query = src_cols * rel_cols[...]
    coef = coefficients(query, (rows_high[...], rows_low[...]), weight[...], at_target, valid)
    query_grad = dot_split((high[...], low[...]), halves(coef), NN)
    pack(rel_out, rel_first[...] + dot_right(rel_hot, halves(query_grad * src_cols), NT))
    state_out[...] = state[...]
    query_out[...] = query
    coef_out[...] = coef
    scaled_out[...] = query_grad * rel_cols[...]


def second_back_kernel(
    moved, spare, spare_state, rows, query, coef, scaled, src_out, src_acc, spare_out, spare_acc
):
    features = spare.shape[0]
    src_hot = as_bf16(onehot(rows[1, 0:1, :], spare.shape[1]))
    src_grad = dot_left(halves(scaled[...]), src_hot, NT)
    src_out[...], src_acc[...] = row_step(
        moved[0:features, :], moved[features : features + 1, :], src_grad
    )
    spare_grad = dot_split(halves(query[...]), halves(coef[...]), NT)
    spare_out[...], spare_acc[...] = row_step(spare[...], spare_state[...], spare_grad)


def relation_kernel(rel, rel_state, *refs):
    terms, (rel_out, state_out) = refs[:-2], refs[-2:]
    total = unpack(tree_sum([term[...] for term in terms]), *rel.shape)
    state = rel_state[...] + total * total
    state_out[...] = state
    rel_out[...] = rel[...] - REL_RATE * total / jnp.sqrt(state)


def call(kernel, in_specs, outs, flops, args, scratch=()):
    shapes = [a if isinstance(a, jax.ShapeDtypeStruct) else jax.ShapeDtypeStruct(a, F32) for a in outs]
    return pl.pallas_call(
        kernel,
        in_specs=in_specs,
        out_specs=[VMEM] * len(outs),
        out_shape=shapes,
        scratch_shapes=list(scratch),
        compiler_params=pltpu.CompilerParams(vmem_limit_bytes=40 * 1024 * 1024),
        cost_estimate=pl.CostEstimate(
            flops=flops, bytes_accessed=sum(a.size * 4 for a in args), transcendentals=0
        ),
    )(*args)


def per_device(
    src_table,
    src_state,
    dst_table,
    dst_state,
    spare_table,
    spare_state,
    relations,
    rel_state,
    edge_rows,
    edge_rel,
    counts,
    negatives,
):
    features, rows = src_table.shape
    edges = edge_rows.shape[2]
    rels = relations.shape[1]
    work = 2 * features * rows * edges
    rel = relations.T
    live = counts.T
    spare_in = swapped(spare_table, "dst", 0)
    operands = [
        src_table, src_state.reshape(1, rows), dst_table, rel, edge_rows, edge_rel, live, negatives,
    ]
    moved_first, query, coef, product = call(
        first_front_kernel,
        [HBM] * 8,
        [(features + 8, rows), (features, edges), (rows, edges), (features, edges)],
        400 * work,
        [pltpu.with_memory_space_constraint(a, pltpu.HBM) for a in operands],
        [pltpu.VMEM(a.shape, a.dtype) for a in operands]
        + [pltpu.SemaphoreType.DMA((len(operands),))],
    )
    moved = passed_along(moved_first, "src", 1)
    dst_next, dst_acc, rel_first, rel_cols, weight, valid, spare_acc = call(
        first_back_kernel,
        [VMEM] * 11,
        [
            (features, rows), (1, rows), (rels, features), (features, edges), (rows, edges),
            (1, edges), (1, rows),
        ],
        3 * work,
        [
            dst_table, dst_state.reshape(1, rows), query, coef, product,
            rel, edge_rows, edge_rel, live, negatives, spare_state.reshape(1, rows),
        ],
    )
    spare_acc_in = swapped(spare_acc, "dst", 0)
    spare_parts = call(
        spare_kernel,
        [VMEM],
        [jax.ShapeDtypeStruct((rows, features), BF16)] * 2
        + [jax.ShapeDtypeStruct((features, rows), BF16)] * 2,
        100 * work,
        [spare_in],
    )
    query, coef, scaled, rel_both, spare_acc_in = call(
        second_front_kernel,
        [VMEM] * 12,
        [
            (features, edges), (rows, edges), (features, edges), packed_shape(rels, features),
            (1, rows),
        ],
        12 * work,
        [
            moved, *spare_parts, rel_cols, weight, valid, edge_rows, edge_rel, rel_first,
            spare_acc_in,
        ],
    )
    src_out, src_state_out, spare_out, spare_state_out = call(
        second_back_kernel,
        [VMEM] * 7,
        [(features, rows), (1, rows), (features, rows), (1, rows)],
        5 * work,
        [moved, spare_in, spare_acc_in, edge_rows, query, coef, scaled],
    )
    terms = exchanged_terms(rel_both)
    relations_out, rel_state_out = call(
        relation_kernel,
        [VMEM] * (2 + len(terms)),
        [(rels, features), (rels, features)],
        rels * features,
        [rel, rel_state.T, *terms],
    )
    return (
        src_out,
        src_state_out.reshape(rows),
        dst_next,
        dst_acc.reshape(rows),
        spare_out,
        spare_state_out.reshape(rows),
        relations_out.T,
        rel_state_out.T,
    )


def solution(mesh):
    in_specs = (
        P(None, ("src", "dst")),
        P(("src", "dst")),
        P(None, ("src", "dst")),
        P(("src", "dst")),
        P(None, ("src", "dst")),
        P(("src", "dst")),
        P(),
        P(),
        P(None, None, ("src", "dst")),
        P(None, ("src", "dst")),
        P(None, ("src", "dst")),
        P(None, ("src", "dst")),
    )
    out_specs = (
        P(None, ("src", "dst")),
        P(("src", "dst")),
        P(None, ("src", "dst")),
        P(("src", "dst")),
        P(None, ("src", "dst")),
        P(("src", "dst")),
        P(),
        P(),
    )
    return jax.shard_map(
        per_device, mesh=mesh, in_specs=in_specs, out_specs=out_specs, check_vma=False
    )
```

```python
import jax
import jax.numpy as jnp
from jax import lax
from jax.experimental import pallas as pl
from jax.experimental.pallas import tpu as pltpu
from jax.sharding import PartitionSpec as P

ROW_RATE = 0.25
REL_RATE = 0.5
NEG_WEIGHT = 0.0625
F32 = jnp.float32
BF16 = jnp.bfloat16
NN = (((1,), (0,)), ((), ()))
NT = (((1,), (1,)), ((), ()))
TN = (((0,), (0,)), ((), ()))
VMEM = pl.BlockSpec(memory_space=pltpu.VMEM)
HBM = pl.BlockSpec(memory_space=pltpu.HBM)


def swapped(array, axis, stride):
    return lax.ppermute(array, axis, [(i, i ^ 1 << stride) for i in range(lax.axis_size(axis))])


def passed_along(array, axis, by):
    count = lax.axis_size(axis)
    return lax.ppermute(array, axis, [(i, (i + by) % count) for i in range(count)])


def sent(array, flips):
    n_src, n_dst = lax.axis_size("src"), lax.axis_size("dst")
    pairs = []
    for u in range(n_src):
        for w in range(n_dst):
            src_flip, dst_flip = flips[u % 2]
            pairs.append((u * n_dst + w, (u ^ src_flip) * n_dst + (w ^ dst_flip)))
    return lax.ppermute(array, ("src", "dst"), pairs)


def core_swapped(array):
    return sent(array, ((1, 0), (1, 0)))


def digits(count, unit):
    steps = []
    while count > 1:
        radix = 4 if count % 4 == 0 else 2
        steps.append((radix, unit))
        count, unit = count // radix, unit * radix
    return steps


def exchanged_terms(array):
    steps = [(0, r, u) for r, u in digits(lax.axis_size("src") // 2, 2)]
    steps += [(1, r, u) for r, u in digits(lax.axis_size("dst"), 1)]
    terms = None
    for axis, radix, unit in steps:

        def flip(k):
            return (0, k * unit) if axis else (k * unit, 0)

        if terms is None:
            one = sent(array, (flip(1), flip(1)))
            array = array + core_swapped(array)
            if radix == 4:
                two = sent(array, (flip(2), flip(2)))
                three = sent(array, (flip(3), flip(3)))
                (late,) = call(add_kernel, [VMEM] * 2, [array.shape], 10**9, [two, three])
                terms = ((array, one + core_swapped(one)), (late,))
            else:
                terms = ((array,), (one + core_swapped(one),))
            continue
        array = tree_sum([tree_sum(pair) for pair in terms])
        if radix == 4:
            odd = sent(array, (flip(1), flip(3)))
            two = sent(array, (flip(2), flip(2)))
            terms = ((array, two), (odd, core_swapped(odd)))
        else:
            terms = ((array,), (sent(array, (flip(1), flip(1))),))
    return [term for pair in terms for term in pair]


def tree_sum(terms):
    terms = list(terms)
    while len(terms) > 1:
        terms = [a + b for a, b in zip(terms[::2], terms[1::2])]
    return terms[0]


def packed_shape(rels, features):
    whole, rest = divmod(features, 128)
    assert rest * rels <= 8 * 128 and rels % 8 == 0
    return (whole * rels + (8 if rest else 0), 128)


def pack(out, values):
    rels, features = values.shape
    whole, rest = divmod(features, 128)
    for k in range(whole):
        out[k * rels : (k + 1) * rels, :] = values[:, k * 128 : (k + 1) * 128]
    if rest:
        tail = [values[8 * k : 8 * (k + 1), whole * 128 :] for k in range(rels // 8)]
        tail.append(jnp.zeros((8, 128 - rest * len(tail)), F32))
        out[whole * rels :, :] = jnp.concatenate(tail, axis=1)


def unpack(packed, rels, features):
    whole, rest = divmod(features, 128)
    parts = [packed[k * rels : (k + 1) * rels, :] for k in range(whole)]
    if rest:
        tail = packed[whole * rels :, :]
        tails = [tail[:, k * rest : (k + 1) * rest] for k in range(rels // 8)]
        parts.append(jnp.concatenate(tails, axis=0))
    return jnp.concatenate(parts, axis=1)


def halves(x):
    high = x.astype(BF16)
    return high, (x - high.astype(F32)).astype(BF16)


def dot(a, b, dims):
    return lax.dot_general(a, b, dims, preferred_element_type=F32)


def dot_split(a, b, dims):
    return dot(a[0], b[0], dims) + dot(a[0], b[1], dims) + dot(a[1], b[0], dims)


def dot_left(a, b, dims):
    return dot(a[0], b, dims) + dot(a[1], b, dims)


def dot_right(a, b, dims):
    return dot(a, b[0], dims) + dot(a, b[1], dims)


def onehot(index, length):
    return index == lax.broadcasted_iota(jnp.int32, (length, index.shape[1]), 0)


def as_bf16(mask):
    return jnp.where(mask, 1.0, 0.0).astype(BF16)


def negative_weight(negatives, rows, edges):
    ones = jnp.ones((negatives.shape[1], edges), BF16)
    return NEG_WEIGHT * dot(as_bf16(onehot(negatives, rows)), ones, NN)


def coefficient_parts(round_id, columns, edge_rows, counts, negatives):
    edges = edge_rows.shape[2]
    weight = negative_weight(negatives[round_id : round_id + 1, :], columns, edges)
    valid = lax.broadcasted_iota(jnp.int32, (1, edges), 1) < counts[:, round_id : round_id + 1]
    hit = jnp.where(onehot(edge_rows[round_id, 1:2, :], columns), 1.0, 0.0)
    scale = jnp.where(valid, 0.5 * (weight + hit), 0.0)
    return scale, scale - jnp.where(valid, hit, 0.0)


def coefficients(query, table_rows, scale, base):
    return scale * jnp.tanh(0.5 * dot_split(table_rows, query, NN)) + base


def row_step(table, state, gradient):
    new_state = state + jnp.sum(gradient * gradient, axis=0, keepdims=True) * (1.0 / table.shape[0])
    return table - gradient * (ROW_RATE / jnp.sqrt(new_state)), new_state


def hot_relations(round_id, edge_rel, rels):
    return as_bf16(onehot(edge_rel[round_id : round_id + 1, :], rels))


def first_front_kernel(
    src_hbm, state_hbm, dst_hbm, rel_hbm, rows_hbm, rels_hbm, counts_hbm, negs_hbm,
    top_out, bottom_out, query_out, coef_out, product_out,
    src, src_state, dst, rel, rows, rels, counts, negs, sems,
):
    pairs = [
        (rows_hbm, rows), (rels_hbm, rels), (rel_hbm, rel), (counts_hbm, counts),
        (negs_hbm, negs), (dst_hbm, dst), (src_hbm, src), (state_hbm, src_state),
    ]
    copies = [pltpu.make_async_copy(a, b, sems.at[i]) for i, (a, b) in enumerate(pairs)]
    for copy in copies:
        copy.start()
    for copy in copies[:5]:
        copy.wait()
    features, columns = src.shape
    src_hot = as_bf16(onehot(rows[0, 0:1, :], columns))
    rel_cols = dot_left(halves(rel[...]), hot_relations(0, rels, rel.shape[0]), TN)
    scale, base = coefficient_parts(0, columns, rows, counts, negs)
    copies[5].wait()
    table_dst = halves(dst[...])
    table_rows = halves(dst[...].T)
    copies[6].wait()
    src_cols = dot_left(halves(src[...]), src_hot, NN)
    query = src_cols * rel_cols
    coef = coefficients(halves(query), table_rows, scale, base)
    query_grad = dot_split(table_dst, halves(coef), NN)
    src_grad = dot_left(halves(query_grad * rel_cols), src_hot, NT)
    copies[7].wait()
    table, state = row_step(src[...], src_state[...], src_grad)
    top, rest = top_out.shape[0], features - top_out.shape[0]
    top_out[...] = table[0:top, :]
    bottom_out[0:rest, :] = table[top:, :]
    bottom_out[rest:, :] = jnp.broadcast_to(state, (bottom_out.shape[0] - rest, columns))
    query_out[...] = query
    coef_out[...] = coef
    product_out[...] = query_grad * src_cols


def first_back_kernel(
    dst, dst_state, query, coef, product, rel, rows, rels, counts, negs,
    spare_state, table_out, state_out, rel_first_out, rel_cols_out, scale_out, base_out, spare_out,
):
    grad = dot_split(halves(query[...]), halves(coef[...]), NT)
    table_out[...], state_out[...] = row_step(dst[...], dst_state[...], grad)
    rel_first_out[...] = dot_right(
        hot_relations(0, rels, rel.shape[0]), halves(product[...]), NT
    )
    rel_cols_out[...] = dot_left(halves(rel[...]), hot_relations(1, rels, rel.shape[0]), TN)
    scale_out[...], base_out[...] = coefficient_parts(1, dst.shape[1], rows, counts, negs)
    spare_out[...] = spare_state[...]


def second_gather_kernel(top, bottom, rel_cols, rows, src_cols_out, high_out, low_out):
    half, features = top.shape[0], rel_cols.shape[0]
    src_hot = as_bf16(onehot(rows[1, 0:1, :], top.shape[1]))
    for low, high, values in ((0, half, top[...]), (half, features, bottom[0 : features - half, :])):
        src_cols = dot_left(halves(values), src_hot, NN)
        src_cols_out[low:high, :] = src_cols
    high_out[...], low_out[...] = halves(src_cols_out[...] * rel_cols[...])


def second_front_kernel(
    spare, src_cols, high, low, rel_cols, scale, base, rels, rel_first, state,
    coef_out, scaled_out, rel_out, state_out,
):
    rel_hot = hot_relations(1, rels, rel_first.shape[0])
    coef = coefficients((high[...], low[...]), halves(spare[...].T), scale[...], base[...])
    query_grad = dot_split(halves(spare[...]), halves(coef), NN)
    pack(rel_out, rel_first[...] + dot_right(rel_hot, halves(query_grad * src_cols[...]), NT))
    state_out[...] = state[...]
    coef_out[...] = coef
    scaled_out[...] = query_grad * rel_cols[...]


def second_back_kernel(
    top, bottom, spare, spare_state, rows, high, low, coef, scaled,
    src_out, src_acc, spare_out, spare_acc,
):
    rest = spare.shape[0] - top.shape[0]
    src_hot = as_bf16(onehot(rows[1, 0:1, :], spare.shape[1]))
    src_grad = dot_left(halves(scaled[...]), src_hot, NT)
    moved = jnp.concatenate([top[...], bottom[0:rest, :]], axis=0)
    src_out[...], src_acc[...] = row_step(moved, bottom[rest : rest + 1, :], src_grad)
    spare_grad = dot_split((high[...], low[...]), halves(coef[...]), NT)
    spare_out[...], spare_acc[...] = row_step(spare[...], spare_state[...], spare_grad)


def add_kernel(left, right, out):
    out[...] = left[...] + right[...]


def relation_kernel(rel, rel_state, *refs):
    terms, (rel_out, state_out) = refs[:-2], refs[-2:]
    total = unpack(tree_sum([term[...] for term in terms]), *rel.shape)
    state = rel_state[...] + total * total
    state_out[...] = state
    rel_out[...] = rel[...] - REL_RATE * total / jnp.sqrt(state)


def call(kernel, in_specs, outs, flops, args, scratch=()):
    shapes = [a if isinstance(a, jax.ShapeDtypeStruct) else jax.ShapeDtypeStruct(a, F32) for a in outs]
    return pl.pallas_call(
        kernel,
        in_specs=in_specs,
        out_specs=[VMEM] * len(outs),
        out_shape=shapes,
        scratch_shapes=list(scratch),
        compiler_params=pltpu.CompilerParams(vmem_limit_bytes=40 * 1024 * 1024),
        cost_estimate=pl.CostEstimate(
            flops=flops, bytes_accessed=sum(a.size * 4 for a in args), transcendentals=0
        ),
    )(*args)


def per_device(
    src_table,
    src_state,
    dst_table,
    dst_state,
    spare_table,
    spare_state,
    relations,
    rel_state,
    edge_rows,
    edge_rel,
    counts,
    negatives,
):
    features, rows = src_table.shape
    edges = edge_rows.shape[2]
    rels = relations.shape[1]
    work = 2 * features * rows * edges
    rel = relations.T
    live = counts.T
    spare_in = swapped(spare_table, "dst", 0)
    operands = [
        src_table, src_state.reshape(1, rows), dst_table, rel, edge_rows, edge_rel, live, negatives,
    ]
    half = features // 16 * 8
    top, bottom, query, coef, product = call(
        first_front_kernel,
        [HBM] * 8,
        [
            (half, rows), (features - half + 8, rows), (features, edges), (rows, edges),
            (features, edges),
        ],
        400 * work,
        [pltpu.with_memory_space_constraint(a, pltpu.HBM) for a in operands],
        [pltpu.VMEM(a.shape, a.dtype) for a in operands]
        + [pltpu.SemaphoreType.DMA((len(operands),))],
    )
    top, bottom = passed_along((top, bottom), "src", 1)
    dst_next, dst_acc, rel_first, rel_cols, scale, base, spare_acc = call(
        first_back_kernel,
        [VMEM] * 11,
        [
            (features, rows), (1, rows), (rels, features), (features, edges), (rows, edges),
            (rows, edges), (1, rows),
        ],
        3 * work,
        [
            dst_table, dst_state.reshape(1, rows), query, coef, product,
            rel, edge_rows, edge_rel, live, negatives, spare_state.reshape(1, rows),
        ],
    )
    spare_acc_in = swapped(spare_acc, "dst", 0)
    src_cols, high, low = call(
        second_gather_kernel,
        [VMEM] * 4,
        [(features, edges)] + [jax.ShapeDtypeStruct((features, edges), BF16)] * 2,
        2 * work,
        [top, bottom, rel_cols, edge_rows],
    )
    coef, scaled, rel_both, spare_acc_in = call(
        second_front_kernel,
        [VMEM] * 10,
        [(rows, edges), (features, edges), packed_shape(rels, features), (1, rows)],
        10 * work,
        [
            spare_in, src_cols, high, low, rel_cols, scale, base, edge_rel, rel_first,
            spare_acc_in,
        ],
    )
    src_out, src_state_out, spare_out, spare_state_out = call(
        second_back_kernel,
        [VMEM] * 9,
        [(features, rows), (1, rows), (features, rows), (1, rows)],
        5 * work,
        [top, bottom, spare_in, spare_acc_in, edge_rows, high, low, coef, scaled],
    )
    terms = exchanged_terms(rel_both)
    relations_out, rel_state_out = call(
        relation_kernel,
        [VMEM] * (2 + len(terms)),
        [(rels, features), (rels, features)],
        rels * features,
        [rel, rel_state.T, *terms],
    )
    return (
        src_out,
        src_state_out.reshape(rows),
        dst_next,
        dst_acc.reshape(rows),
        spare_out,
        spare_state_out.reshape(rows),
        relations_out.T,
        rel_state_out.T,
    )


def solution(mesh):
    in_specs = (
        P(None, ("src", "dst")),
        P(("src", "dst")),
        P(None, ("src", "dst")),
        P(("src", "dst")),
        P(None, ("src", "dst")),
        P(("src", "dst")),
        P(),
        P(),
        P(None, None, ("src", "dst")),
        P(None, ("src", "dst")),
        P(None, ("src", "dst")),
        P(None, ("src", "dst")),
    )
    out_specs = (
        P(None, ("src", "dst")),
        P(("src", "dst")),
        P(None, ("src", "dst")),
        P(("src", "dst")),
        P(None, ("src", "dst")),
        P(("src", "dst")),
        P(),
        P(),
    )
    return jax.shard_map(
        per_device, mesh=mesh, in_specs=in_specs, out_specs=out_specs, check_vma=False
    )
```

```python
import functools

import jax
import jax.numpy as jnp
from jax import lax
from jax.experimental import pallas as pl
from jax.experimental.pallas import tpu as pltpu
from jax.sharding import PartitionSpec as P

ROW_RATE = 0.25
REL_RATE = 0.5
NEG_WEIGHT = 0.0625
F32 = jnp.float32
BF16 = jnp.bfloat16
NN = (((1,), (0,)), ((), ()))
NT = (((1,), (1,)), ((), ()))
TN = (((0,), (0,)), ((), ()))
VMEM = pl.BlockSpec(memory_space=pltpu.VMEM)
HBM = pl.BlockSpec(memory_space=pltpu.HBM)


def swapped(array, axis, stride):
    return lax.ppermute(array, axis, [(i, i ^ 1 << stride) for i in range(lax.axis_size(axis))])


def passed_along(array, axis, by):
    count = lax.axis_size(axis)
    return lax.ppermute(array, axis, [(i, (i + by) % count) for i in range(count)])


def sent(array, flips):
    n_src, n_dst = lax.axis_size("src"), lax.axis_size("dst")
    pairs = []
    for u in range(n_src):
        for w in range(n_dst):
            src_flip, dst_flip = flips[u % 2]
            pairs.append((u * n_dst + w, (u ^ src_flip) * n_dst + (w ^ dst_flip)))
    return lax.ppermute(array, ("src", "dst"), pairs)


def core_swapped(array):
    return sent(array, ((1, 0), (1, 0)))


def digits(count, unit):
    steps = []
    while count > 1:
        radix = 4 if count % 4 == 0 else 2
        steps.append((radix, unit))
        count, unit = count // radix, unit * radix
    return steps


def exchanged_terms(array):
    steps = [(0, r, u) for r, u in digits(lax.axis_size("src") // 2, 2)]
    steps += [(1, r, u) for r, u in digits(lax.axis_size("dst"), 1)]
    terms = None
    for axis, radix, unit in steps:

        def flip(k):
            return (0, k * unit) if axis else (k * unit, 0)

        if terms is None:
            one = sent(array, (flip(1), flip(1)))
            array = array + core_swapped(array)
            if radix == 4:
                two = sent(array, (flip(2), flip(2)))
                three = sent(array, (flip(3), flip(3)))
                (late,) = call(add_kernel, [VMEM] * 2, [array.shape], 10**9, [two, three])
                terms = ((array, one + core_swapped(one)), (late,))
            else:
                terms = ((array,), (one + core_swapped(one),))
            continue
        array = tree_sum([tree_sum(pair) for pair in terms])
        if radix == 4:
            odd = sent(array, (flip(1), flip(3)))
            two = sent(array, (flip(2), flip(2)))
            terms = ((array, two), (odd, core_swapped(odd)))
        else:
            terms = ((array,), (sent(array, (flip(1), flip(1))),))
    return [term for pair in terms for term in pair]


def tree_sum(terms):
    terms = list(terms)
    while len(terms) > 1:
        terms = [a + b for a, b in zip(terms[::2], terms[1::2])]
    return terms[0]


def packed_shape(rels, features):
    whole, rest = divmod(features, 128)
    assert rest * rels <= 8 * 128 and rels % 8 == 0
    return (whole * rels + (8 if rest else 0), 128)


def pack(out, values):
    rels, features = values.shape
    whole, rest = divmod(features, 128)
    for k in range(whole):
        out[k * rels : (k + 1) * rels, :] = values[:, k * 128 : (k + 1) * 128]
    if rest:
        tail = [values[8 * k : 8 * (k + 1), whole * 128 :] for k in range(rels // 8)]
        tail.append(jnp.zeros((8, 128 - rest * len(tail)), F32))
        out[whole * rels :, :] = jnp.concatenate(tail, axis=1)


def unpack(packed, rels, features):
    whole, rest = divmod(features, 128)
    parts = [packed[k * rels : (k + 1) * rels, :] for k in range(whole)]
    if rest:
        tail = packed[whole * rels :, :]
        tails = [tail[:, k * rest : (k + 1) * rest] for k in range(rels // 8)]
        parts.append(jnp.concatenate(tails, axis=0))
    return jnp.concatenate(parts, axis=1)


def halves(x):
    high = x.astype(BF16)
    return high, (x - high.astype(F32)).astype(BF16)


def dot(a, b, dims):
    return lax.dot_general(a, b, dims, preferred_element_type=F32)


def stacked(parts, dims, side):
    return jnp.concatenate(parts, axis=dims[0][side][0])


def dot_split(a, b, dims):
    if a[0].shape[dims[0][0][0]] % 128:
        return dot(a[0], b[0], dims) + dot(a[0], b[1], dims) + dot(a[1], b[0], dims)
    left = stacked((a[0], a[0], a[1]), dims, 0)
    return dot(left, stacked((b[0], b[1], b[0]), dims, 1), dims)


def dot_left(a, b, dims):
    if a[0].shape[dims[0][0][0]] % 128:
        return dot(a[0], b, dims) + dot(a[1], b, dims)
    return dot(stacked(a, dims, 0), stacked((b, b), dims, 1), dims)


def dot_right(a, b, dims):
    if b[0].shape[dims[0][1][0]] % 128:
        return dot(a, b[0], dims) + dot(a, b[1], dims)
    return dot(stacked((a, a), dims, 0), stacked(b, dims, 1), dims)


def onehot(index, length):
    return index == lax.broadcasted_iota(jnp.int32, (length, index.shape[1]), 0)


def as_bf16(mask):
    return jnp.where(mask, 1.0, 0.0).astype(BF16)


def negative_weight(negatives, rows, edges):
    ones = jnp.ones((negatives.shape[1], edges), BF16)
    return NEG_WEIGHT * dot(as_bf16(onehot(negatives, rows)), ones, NN)


def coefficient_parts(round_id, columns, edge_rows, counts, negatives):
    edges = edge_rows.shape[2]
    weight = negative_weight(negatives[round_id : round_id + 1, :], columns, edges)
    valid = lax.broadcasted_iota(jnp.int32, (1, edges), 1) < counts[:, round_id : round_id + 1]
    hit = jnp.where(onehot(edge_rows[round_id, 1:2, :], columns), 1.0, 0.0)
    scale = jnp.where(valid, 0.5 * (weight + hit), 0.0)
    return scale, scale - jnp.where(valid, hit, 0.0)


def coefficients(query, table_rows, scale, base):
    return scale * jnp.tanh(0.5 * dot_split(table_rows, query, NN)) + base


def row_step(table, state, gradient):
    new_state = state + jnp.sum(gradient * gradient, axis=0, keepdims=True) * (1.0 / table.shape[0])
    return table - gradient * (ROW_RATE / jnp.sqrt(new_state)), new_state


def hot_relations(round_id, edge_rel, rels):
    return as_bf16(onehot(edge_rel[round_id : round_id + 1, :], rels))


def core_of_chip():
    return lax.rem(lax.axis_index("src"), 2)


def first_front_kernel(core, *refs):
    given, refs = (refs[:3], refs[3:]) if core == 0 else ((), refs)

    @pl.when(core_of_chip() == core)
    def _():
        first_front(*refs)

    if given:

        @pl.when(core_of_chip() != core)
        def _():
            for value, out in zip(given, refs[-12:-9]):
                out[...] = value[...]


def first_front(
    src_hbm, state_hbm, dst_hbm, rel_hbm, rows_hbm, rels_hbm, counts_hbm, negs_hbm, *refs
):
    *moved_outs, query_out, coef_out, product_out = refs[:-9]
    src, src_state, dst, rel, rows, rels, counts, negs, sems = refs[-9:]
    features, columns = src.shape
    small = [
        (rows_hbm, rows), (rels_hbm, rels), (rel_hbm, rel), (counts_hbm, counts), (negs_hbm, negs),
    ]
    slabs = [(dst_hbm, dst), (src_hbm, src)]
    pairs = small + slabs + [(state_hbm, src_state)]
    copies = [pltpu.make_async_copy(a, b, sems.at[i]) for i, (a, b) in enumerate(pairs)]
    for copy in copies:
        copy.start()
    for_dst, for_src, for_state = copies[len(small) :]
    for copy in copies[: len(small)]:
        copy.wait()
    src_hot = as_bf16(onehot(rows[0, 0:1, :], columns))
    rel_cols = dot_left(halves(rel[...]), hot_relations(0, rels, rel.shape[0]), TN)
    scale, base = coefficient_parts(0, columns, rows, counts, negs)
    for_dst.wait()
    table_dst = halves(dst[...])
    table_rows = halves(dst[...].T)
    for_src.wait()
    src_cols = dot_left(halves(src[...]), src_hot, NN)
    query = src_cols * rel_cols
    coef = coefficients(halves(query), table_rows, scale, base)
    query_grad = dot_split(table_dst, halves(coef), NN)
    src_grad = dot_left(halves(query_grad * rel_cols), src_hot, NT)
    for_state.wait()
    table, state = row_step(src[...], src_state[...], src_grad)
    moved = jnp.concatenate([table, jnp.broadcast_to(state, (24, columns))], axis=0)
    low = 0
    for out in moved_outs:
        out[...] = moved[low : low + out.shape[0], :]
        low += out.shape[0]
    query_out[...] = query
    coef_out[...] = coef
    product_out[...] = query_grad * src_cols


def first_back_kernel(
    dst, dst_state, query, coef, product, rel, rows, rels, counts, negs,
    spare_state, table_out, state_out, rel_first_out, rel_cols_out, scale_out, base_out, spare_out,
):
    grad = dot_split(halves(query[...]), halves(coef[...]), NT)
    table_out[...], state_out[...] = row_step(dst[...], dst_state[...], grad)
    rel_first_out[...] = dot_right(
        hot_relations(0, rels, rel.shape[0]), halves(product[...]), NT
    )
    rel_cols_out[...] = dot_left(halves(rel[...]), hot_relations(1, rels, rel.shape[0]), TN)
    scale_out[...], base_out[...] = coefficient_parts(1, dst.shape[1], rows, counts, negs)
    spare_out[...] = spare_state[...]


def second_gather_kernel(count, *refs):
    across, within = refs[:count], refs[count:-6]
    rel_cols, rows, moved_out, src_cols_out, high_out, low_out = refs[-6:]
    moved = jnp.where(
        core_of_chip() == 0,
        jnp.concatenate([part[...] for part in across], axis=0)[0 : moved_out.shape[0], :],
        jnp.concatenate([part[...] for part in within], axis=0)[0 : moved_out.shape[0], :],
    )
    features, columns = src_cols_out.shape[0], moved.shape[1]
    src_hot = as_bf16(onehot(rows[1, 0:1, :], columns))
    src_cols = dot_left(halves(moved[0:features, :]), src_hot, NN)
    high_out[...], low_out[...] = halves(src_cols * rel_cols[...])
    src_cols_out[...] = src_cols
    moved_out[...] = moved


def second_front_kernel(
    spare, src_cols, high, low, rel_cols, scale, base, rels, rel_first, state,
    coef_out, scaled_out, rel_out, state_out,
):
    rel_hot = hot_relations(1, rels, rel_first.shape[0])
    coef = coefficients((high[...], low[...]), halves(spare[...].T), scale[...], base[...])
    query_grad = dot_split(halves(spare[...]), halves(coef), NN)
    pack(rel_out, rel_first[...] + dot_right(rel_hot, halves(query_grad * src_cols[...]), NT))
    state_out[...] = state[...]
    coef_out[...] = coef
    scaled_out[...] = query_grad * rel_cols[...]


def second_back_kernel(
    moved, spare, spare_state, rows, high, low, coef, scaled,
    src_out, src_acc, spare_out, spare_acc,
):
    features = spare.shape[0]
    src_hot = as_bf16(onehot(rows[1, 0:1, :], spare.shape[1]))
    src_grad = dot_left(halves(scaled[...]), src_hot, NT)
    src_out[...], src_acc[...] = row_step(
        moved[0:features, :], moved[features : features + 1, :], src_grad
    )
    spare_grad = dot_split((high[...], low[...]), halves(coef[...]), NT)
    spare_out[...], spare_acc[...] = row_step(spare[...], spare_state[...], spare_grad)


def add_kernel(left, right, out):
    out[...] = left[...] + right[...]


def relation_kernel(rel, rel_state, *refs):
    terms, (rel_out, state_out) = refs[:-2], refs[-2:]
    total = unpack(tree_sum([term[...] for term in terms]), *rel.shape)
    state = rel_state[...] + total * total
    state_out[...] = state
    rel_out[...] = rel[...] - REL_RATE * total / jnp.sqrt(state)


def call(kernel, in_specs, outs, flops, args, scratch=()):
    shapes = [a if isinstance(a, jax.ShapeDtypeStruct) else jax.ShapeDtypeStruct(a, F32) for a in outs]
    return pl.pallas_call(
        kernel,
        in_specs=in_specs,
        out_specs=[VMEM] * len(outs),
        out_shape=shapes,
        scratch_shapes=list(scratch),
        compiler_params=pltpu.CompilerParams(vmem_limit_bytes=40 * 1024 * 1024),
        cost_estimate=pl.CostEstimate(
            flops=flops, bytes_accessed=sum(a.size * 4 for a in args), transcendentals=0
        ),
    )(*args)


def cut(length, parts):
    step = -(-length // (8 * parts)) * 8
    return [min(step, length - low) for low in range(0, length, step)]


def per_device(
    src_table,
    src_state,
    dst_table,
    dst_state,
    spare_table,
    spare_state,
    relations,
    rel_state,
    edge_rows,
    edge_rel,
    counts,
    negatives,
):
    features, rows = src_table.shape
    edges = edge_rows.shape[2]
    rels = relations.shape[1]
    work = 2 * features * rows * edges
    rel = relations.T
    live = counts.T
    spare_in = swapped(spare_table, "dst", 0)
    operands = [
        src_table, src_state.reshape(1, rows), dst_table, rel, edge_rows, edge_rel, live, negatives,
    ]
    hbm = [pltpu.with_memory_space_constraint(a, pltpu.HBM) for a in operands]

    def first_on(core, pieces, cost, given=()):
        return call(
            functools.partial(first_front_kernel, core),
            [VMEM] * len(given) + [HBM] * 8,
            [(size, rows) for size in pieces] + [(features, edges), (rows, edges), (features, edges)],
            cost,
            [*given, *hbm],
            [pltpu.VMEM(a.shape, a.dtype) for a in operands]
            + [pltpu.SemaphoreType.DMA((len(operands),))],
        )

    *across, query, coef, product = first_on(1, cut(features + 24, 2), 400 * work)
    across = passed_along(tuple(across), "src", 1)
    *within, query, coef, product = first_on(
        0, cut(features + 8, 2), 1 * work, (query, coef, product)
    )
    within = tuple(core_swapped(part) for part in within)
    dst_next, dst_acc, rel_first, rel_cols, scale, base, spare_acc = call(
        first_back_kernel,
        [VMEM] * 11,
        [
            (features, rows), (1, rows), (rels, features), (features, edges), (rows, edges),
            (rows, edges), (1, rows),
        ],
        3 * work,
        [
            dst_table, dst_state.reshape(1, rows), query, coef, product,
            rel, edge_rows, edge_rel, live, negatives, spare_state.reshape(1, rows),
        ],
    )
    spare_acc_in = swapped(spare_acc, "dst", 0)
    moved, src_cols, high, low = call(
        functools.partial(second_gather_kernel, len(across)),
        [VMEM] * (len(across) + len(within) + 2),
        [(features + 8, rows), (features, edges)] + [jax.ShapeDtypeStruct((features, edges), BF16)] * 2,
        2 * work,
        [*across, *within, rel_cols, edge_rows],
    )
    coef, scaled, rel_both, spare_acc_in = call(
        second_front_kernel,
        [VMEM] * 10,
        [(rows, edges), (features, edges), packed_shape(rels, features), (1, rows)],
        10 * work,
        [
            spare_in, src_cols, high, low, rel_cols, scale, base, edge_rel, rel_first,
            spare_acc_in,
        ],
    )
    src_out, src_state_out, spare_out, spare_state_out = call(
        second_back_kernel,
        [VMEM] * 8,
        [(features, rows), (1, rows), (features, rows), (1, rows)],
        5 * work,
        [moved, spare_in, spare_acc_in, edge_rows, high, low, coef, scaled],
    )
    terms = exchanged_terms(rel_both)
    relations_out, rel_state_out = call(
        relation_kernel,
        [VMEM] * (2 + len(terms)),
        [(rels, features), (rels, features)],
        rels * features,
        [rel, rel_state.T, *terms],
    )
    return (
        src_out,
        src_state_out.reshape(rows),
        dst_next,
        dst_acc.reshape(rows),
        spare_out,
        spare_state_out.reshape(rows),
        relations_out.T,
        rel_state_out.T,
    )


def solution(mesh):
    in_specs = (
        P(None, ("src", "dst")),
        P(("src", "dst")),
        P(None, ("src", "dst")),
        P(("src", "dst")),
        P(None, ("src", "dst")),
        P(("src", "dst")),
        P(),
        P(),
        P(None, None, ("src", "dst")),
        P(None, ("src", "dst")),
        P(None, ("src", "dst")),
        P(None, ("src", "dst")),
    )
    out_specs = (
        P(None, ("src", "dst")),
        P(("src", "dst")),
        P(None, ("src", "dst")),
        P(("src", "dst")),
        P(None, ("src", "dst")),
        P(("src", "dst")),
        P(),
        P(),
    )
    return jax.shard_map(
        per_device, mesh=mesh, in_specs=in_specs, out_specs=out_specs, check_vma=False
    )
```

```python
import functools

import jax
import jax.numpy as jnp
from jax import lax
from jax.experimental import pallas as pl
from jax.experimental.pallas import tpu as pltpu
from jax.sharding import PartitionSpec as P

ROW_RATE = 0.25
REL_RATE = 0.5
NEG_WEIGHT = 0.0625
F32 = jnp.float32
BF16 = jnp.bfloat16
NN = (((1,), (0,)), ((), ()))
NT = (((1,), (1,)), ((), ()))
TN = (((0,), (0,)), ((), ()))
VMEM = pl.BlockSpec(memory_space=pltpu.VMEM)
HBM = pl.BlockSpec(memory_space=pltpu.HBM)


def swapped(array, axis, stride):
    return lax.ppermute(array, axis, [(i, i ^ 1 << stride) for i in range(lax.axis_size(axis))])


def passed_along(array, axis, by):
    count = lax.axis_size(axis)
    return lax.ppermute(array, axis, [(i, (i + by) % count) for i in range(count)])


def sent(array, flips):
    n_src, n_dst = lax.axis_size("src"), lax.axis_size("dst")
    pairs = []
    for u in range(n_src):
        for w in range(n_dst):
            src_flip, dst_flip = flips[u % 2]
            pairs.append((u * n_dst + w, (u ^ src_flip) * n_dst + (w ^ dst_flip)))
    return lax.ppermute(array, ("src", "dst"), pairs)


def core_swapped(array):
    return sent(array, ((1, 0), (1, 0)))


def digits(count, unit):
    steps = []
    while count > 1:
        radix = 4 if count % 4 == 0 else 2
        steps.append((radix, unit))
        count, unit = count // radix, unit * radix
    return steps


def exchanged_terms(array, beside):
    steps = [(0, r, u) for r, u in digits(lax.axis_size("src") // 2, 2)]
    steps += [(1, r, u) for r, u in digits(lax.axis_size("dst"), 1)]
    terms = None
    for axis, radix, unit in steps:

        def flip(k):
            return (0, k * unit) if axis else (k * unit, 0)

        if terms is None:
            one = sent(array, (flip(1), flip(1)))
            array = array + core_swapped(array)
            if radix == 4:
                two = sent(array, (flip(2), flip(2)))
                three = sent(array, (flip(3), flip(3)))
                turn = beside(one)
                (late,) = call(add_kernel, [VMEM] * 3, [array.shape], 10**9, [two, three, turn])
                terms = ((array, one + core_swapped(one)), (late,))
            else:
                beside(one)
                terms = ((array,), (one + core_swapped(one),))
            continue
        array = tree_sum([tree_sum(pair) for pair in terms])
        if radix == 4:
            odd = sent(array, (flip(1), flip(3)))
            two = sent(array, (flip(2), flip(2)))
            terms = ((array, two), (odd, core_swapped(odd)))
        else:
            terms = ((array,), (sent(array, (flip(1), flip(1))),))
    return [term for pair in terms for term in pair]


def tree_sum(terms):
    terms = list(terms)
    while len(terms) > 1:
        terms = [a + b for a, b in zip(terms[::2], terms[1::2])]
    return terms[0]


def packed_shape(rels, features):
    whole, rest = divmod(features, 128)
    assert rest * rels <= 8 * 128 and rels % 8 == 0
    return (whole * rels + (8 if rest else 0), 128)


def pack(out, values):
    rels, features = values.shape
    whole, rest = divmod(features, 128)
    for k in range(whole):
        out[k * rels : (k + 1) * rels, :] = values[:, k * 128 : (k + 1) * 128]
    if rest:
        tail = [values[8 * k : 8 * (k + 1), whole * 128 :] for k in range(rels // 8)]
        tail.append(jnp.zeros((8, 128 - rest * len(tail)), F32))
        out[whole * rels :, :] = jnp.concatenate(tail, axis=1)


def unpack(packed, rels, features):
    whole, rest = divmod(features, 128)
    parts = [packed[k * rels : (k + 1) * rels, :] for k in range(whole)]
    if rest:
        tail = packed[whole * rels :, :]
        tails = [tail[:, k * rest : (k + 1) * rest] for k in range(rels // 8)]
        parts.append(jnp.concatenate(tails, axis=0))
    return jnp.concatenate(parts, axis=1)


def halves(x):
    high = x.astype(BF16)
    return high, (x - high.astype(F32)).astype(BF16)


def dot(a, b, dims):
    return lax.dot_general(a, b, dims, preferred_element_type=F32)


def stacked(parts, dims, side):
    return jnp.concatenate(parts, axis=dims[0][side][0])


def dot_split(a, b, dims):
    if a[0].shape[dims[0][0][0]] % 128:
        return dot(a[0], b[0], dims) + dot(a[0], b[1], dims) + dot(a[1], b[0], dims)
    left = stacked((a[0], a[0], a[1]), dims, 0)
    return dot(left, stacked((b[0], b[1], b[0]), dims, 1), dims)


def dot_left(a, b, dims):
    if a[0].shape[dims[0][0][0]] % 128:
        return dot(a[0], b, dims) + dot(a[1], b, dims)
    return dot(stacked(a, dims, 0), stacked((b, b), dims, 1), dims)


def dot_right(a, b, dims):
    if b[0].shape[dims[0][1][0]] % 128:
        return dot(a, b[0], dims) + dot(a, b[1], dims)
    return dot(stacked((a, a), dims, 0), stacked(b, dims, 1), dims)


def onehot(index, length):
    return index == lax.broadcasted_iota(jnp.int32, (length, index.shape[1]), 0)


def as_bf16(mask):
    return jnp.where(mask, 1.0, 0.0).astype(BF16)


def negative_weight(negatives, rows, edges):
    ones = jnp.ones((negatives.shape[1], edges), BF16)
    return NEG_WEIGHT * dot(as_bf16(onehot(negatives, rows)), ones, NN)


def coefficient_parts(round_id, columns, edge_rows, counts, negatives):
    edges = edge_rows.shape[2]
    weight = negative_weight(negatives[round_id : round_id + 1, :], columns, edges)
    valid = lax.broadcasted_iota(jnp.int32, (1, edges), 1) < counts[:, round_id : round_id + 1]
    hit = jnp.where(onehot(edge_rows[round_id, 1:2, :], columns), 1.0, 0.0)
    scale = jnp.where(valid, 0.5 * (weight + hit), 0.0)
    return scale, scale - jnp.where(valid, hit, 0.0)


def coefficients(query, table_rows, scale, base):
    return scale * jnp.tanh(0.5 * dot_split(table_rows, query, NN)) + base


def row_step(table, state, gradient):
    new_state = state + jnp.sum(gradient * gradient, axis=0, keepdims=True) * (1.0 / table.shape[0])
    return table - gradient * (ROW_RATE / jnp.sqrt(new_state)), new_state


def hot_relations(round_id, edge_rel, rels):
    return as_bf16(onehot(edge_rel[round_id : round_id + 1, :], rels))


def core_of_chip():
    return lax.rem(lax.axis_index("src"), 2)


def first_front_kernel(core, *refs):
    given, refs = (refs[:3], refs[3:]) if core == 0 else ((), refs)

    @pl.when(core_of_chip() == core)
    def _():
        first_front(*refs)

    if given:

        @pl.when(core_of_chip() != core)
        def _():
            for value, out in zip(given, refs[-12:-9]):
                out[...] = value[...]


def first_front(
    src_hbm, state_hbm, dst_hbm, rel_hbm, rows_hbm, rels_hbm, counts_hbm, negs_hbm, *refs
):
    *moved_outs, query_out, coef_out, product_out = refs[:-9]
    src, src_state, dst, rel, rows, rels, counts, negs, sems = refs[-9:]
    features, columns = src.shape
    small = [
        (rows_hbm, rows), (rels_hbm, rels), (rel_hbm, rel), (counts_hbm, counts), (negs_hbm, negs),
    ]
    slabs = [(dst_hbm, dst), (src_hbm, src)]
    pairs = small + slabs + [(state_hbm, src_state)]
    copies = [pltpu.make_async_copy(a, b, sems.at[i]) for i, (a, b) in enumerate(pairs)]
    for copy in copies:
        copy.start()
    for_dst, for_src, for_state = copies[len(small) :]
    for copy in copies[: len(small)]:
        copy.wait()
    src_hot = as_bf16(onehot(rows[0, 0:1, :], columns))
    rel_cols = dot_left(halves(rel[...]), hot_relations(0, rels, rel.shape[0]), TN)
    scale, base = coefficient_parts(0, columns, rows, counts, negs)
    for_dst.wait()
    table_dst = halves(dst[...])
    table_rows = halves(dst[...].T)
    for_src.wait()
    src_cols = dot_left(halves(src[...]), src_hot, NN)
    query = src_cols * rel_cols
    coef = coefficients(halves(query), table_rows, scale, base)
    query_grad = dot_split(table_dst, halves(coef), NN)
    src_grad = dot_left(halves(query_grad * rel_cols), src_hot, NT)
    for_state.wait()
    table, state = row_step(src[...], src_state[...], src_grad)
    moved = jnp.concatenate([table, jnp.broadcast_to(state, (24, columns))], axis=0)
    low = 0
    for out in moved_outs:
        out[...] = moved[low : low + out.shape[0], :]
        low += out.shape[0]
    query_out[...] = query
    coef_out[...] = coef
    product_out[...] = query_grad * src_cols


def between_kernel(
    product, rel, rows, rels, counts, negs, spare_state,
    rel_first_out, rel_cols_out, scale_out, base_out, spare_out,
):
    rel_first_out[...] = dot_right(
        hot_relations(0, rels, rel.shape[0]), halves(product[...]), NT
    )
    rel_cols_out[...] = dot_left(halves(rel[...]), hot_relations(1, rels, rel.shape[0]), TN)
    columns = scale_out.shape[0]
    scale_out[...], base_out[...] = coefficient_parts(1, columns, rows, counts, negs)
    spare_out[...] = spare_state[...]


def first_back_kernel(dst, dst_state, query, coef, turn, table_out, state_out, turn_out):
    grad = dot_split(halves(query[...]), halves(coef[...]), NT)
    table_out[...], state_out[...] = row_step(dst[...], dst_state[...], grad)
    turn_out[...] = jnp.zeros_like(turn_out)


def second_gather_kernel(count, *refs):
    across, within = refs[:count], refs[count:-6]
    rel_cols, rows, moved_out, src_cols_out, high_out, low_out = refs[-6:]
    moved = jnp.where(
        core_of_chip() == 0,
        jnp.concatenate([part[...] for part in across], axis=0)[0 : moved_out.shape[0], :],
        jnp.concatenate([part[...] for part in within], axis=0)[0 : moved_out.shape[0], :],
    )
    features, columns = src_cols_out.shape[0], moved.shape[1]
    src_hot = as_bf16(onehot(rows[1, 0:1, :], columns))
    src_cols = dot_left(halves(moved[0:features, :]), src_hot, NN)
    high_out[...], low_out[...] = halves(src_cols * rel_cols[...])
    src_cols_out[...] = src_cols
    moved_out[...] = moved


def second_front_kernel(
    spare, src_cols, high, low, rel_cols, scale, base, rels, rel_first, state,
    coef_out, scaled_out, rel_out, state_out,
):
    rel_hot = hot_relations(1, rels, rel_first.shape[0])
    coef = coefficients((high[...], low[...]), halves(spare[...].T), scale[...], base[...])
    query_grad = dot_split(halves(spare[...]), halves(coef), NN)
    pack(rel_out, rel_first[...] + dot_right(rel_hot, halves(query_grad * src_cols[...]), NT))
    state_out[...] = state[...]
    coef_out[...] = coef
    scaled_out[...] = query_grad * rel_cols[...]


def second_back_kernel(
    moved, spare, spare_state, rows, high, low, coef, scaled,
    src_out, src_acc, spare_out, spare_acc,
):
    features = spare.shape[0]
    src_hot = as_bf16(onehot(rows[1, 0:1, :], spare.shape[1]))
    src_grad = dot_left(halves(scaled[...]), src_hot, NT)
    src_out[...], src_acc[...] = row_step(
        moved[0:features, :], moved[features : features + 1, :], src_grad
    )
    spare_grad = dot_split((high[...], low[...]), halves(coef[...]), NT)
    spare_out[...], spare_acc[...] = row_step(spare[...], spare_state[...], spare_grad)


def add_kernel(left, right, turn, out):
    out[...] = left[...] + right[...]


def relation_kernel(rel, rel_state, *refs):
    terms, (rel_out, state_out) = refs[:-2], refs[-2:]
    total = unpack(tree_sum([term[...] for term in terms]), *rel.shape)
    state = rel_state[...] + total * total
    state_out[...] = state
    rel_out[...] = rel[...] - REL_RATE * total / jnp.sqrt(state)


def call(kernel, in_specs, outs, flops, args, scratch=()):
    shapes = [a if isinstance(a, jax.ShapeDtypeStruct) else jax.ShapeDtypeStruct(a, F32) for a in outs]
    return pl.pallas_call(
        kernel,
        in_specs=in_specs,
        out_specs=[VMEM] * len(outs),
        out_shape=shapes,
        scratch_shapes=list(scratch),
        compiler_params=pltpu.CompilerParams(vmem_limit_bytes=40 * 1024 * 1024),
        cost_estimate=pl.CostEstimate(
            flops=flops, bytes_accessed=sum(a.size * 4 for a in args), transcendentals=0
        ),
    )(*args)


def cut(length, parts):
    step = -(-length // (8 * parts)) * 8
    return [min(step, length - low) for low in range(0, length, step)]


def per_device(
    src_table,
    src_state,
    dst_table,
    dst_state,
    spare_table,
    spare_state,
    relations,
    rel_state,
    edge_rows,
    edge_rel,
    counts,
    negatives,
):
    features, rows = src_table.shape
    edges = edge_rows.shape[2]
    rels = relations.shape[1]
    work = 2 * features * rows * edges
    rel = relations.T
    live = counts.T
    spare_in = swapped(spare_table, "dst", 0)
    operands = [
        src_table, src_state.reshape(1, rows), dst_table, rel, edge_rows, edge_rel, live, negatives,
    ]
    hbm = [pltpu.with_memory_space_constraint(a, pltpu.HBM) for a in operands]

    def first_on(core, pieces, cost, given=()):
        return call(
            functools.partial(first_front_kernel, core),
            [VMEM] * len(given) + [HBM] * 8,
            [(size, rows) for size in pieces] + [(features, edges), (rows, edges), (features, edges)],
            cost,
            [*given, *hbm],
            [pltpu.VMEM(a.shape, a.dtype) for a in operands]
            + [pltpu.SemaphoreType.DMA((len(operands),))],
        )

    *across, query, coef, product = first_on(1, cut(features + 24, 2), 400 * work)
    across = passed_along(tuple(across), "src", 1)
    *within, query, coef_first, product = first_on(
        0, cut(features + 8, 2), 1 * work, (query, coef, product)
    )
    within = tuple(core_swapped(part) for part in within)
    rel_first, rel_cols, scale, base, spare_acc = call(
        between_kernel,
        [VMEM] * 7,
        [(rels, features), (features, edges), (rows, edges), (rows, edges), (1, rows)],
        work,
        [product, rel, edge_rows, edge_rel, live, negatives, spare_state.reshape(1, rows)],
    )
    spare_acc_in = swapped(spare_acc, "dst", 0)
    moved, src_cols, high, low = call(
        functools.partial(second_gather_kernel, len(across)),
        [VMEM] * (len(across) + len(within) + 2),
        [(features + 8, rows), (features, edges)] + [jax.ShapeDtypeStruct((features, edges), BF16)] * 2,
        2 * work,
        [*across, *within, rel_cols, edge_rows],
    )
    coef, scaled, rel_both, spare_acc_in = call(
        second_front_kernel,
        [VMEM] * 10,
        [(rows, edges), (features, edges), packed_shape(rels, features), (1, rows)],
        10 * work,
        [
            spare_in, src_cols, high, low, rel_cols, scale, base, edge_rel, rel_first,
            spare_acc_in,
        ],
    )
    src_out, src_state_out, spare_out, spare_state_out = call(
        second_back_kernel,
        [VMEM] * 8,
        [(features, rows), (1, rows), (features, rows), (1, rows)],
        5 * work,
        [moved, spare_in, spare_acc_in, edge_rows, high, low, coef, scaled],
    )
    dst_results = []

    def first_back(one):
        dst_results.extend(
            call(
                first_back_kernel,
                [VMEM] * 5,
                [(features, rows), (1, rows), (8, 128)],
                3 * work,
                [dst_table, dst_state.reshape(1, rows), query, coef_first, one],
            )
        )
        return dst_results.pop()

    terms = exchanged_terms(rel_both, first_back)
    dst_next, dst_acc = dst_results
    relations_out, rel_state_out = call(
        relation_kernel,
        [VMEM] * (2 + len(terms)),
        [(rels, features), (rels, features)],
        rels * features,
        [rel, rel_state.T, *terms],
    )
    return (
        src_out,
        src_state_out.reshape(rows),
        dst_next,
        dst_acc.reshape(rows),
        spare_out,
        spare_state_out.reshape(rows),
        relations_out.T,
        rel_state_out.T,
    )


def solution(mesh):
    in_specs = (
        P(None, ("src", "dst")),
        P(("src", "dst")),
        P(None, ("src", "dst")),
        P(("src", "dst")),
        P(None, ("src", "dst")),
        P(("src", "dst")),
        P(),
        P(),
        P(None, None, ("src", "dst")),
        P(None, ("src", "dst")),
        P(None, ("src", "dst")),
        P(None, ("src", "dst")),
    )
    out_specs = (
        P(None, ("src", "dst")),
        P(("src", "dst")),
        P(None, ("src", "dst")),
        P(("src", "dst")),
        P(None, ("src", "dst")),
        P(("src", "dst")),
        P(),
        P(),
    )
    return jax.shard_map(
        per_device, mesh=mesh, in_specs=in_specs, out_specs=out_specs, check_vma=False
    )
```

```python
import jax
import jax.numpy as jnp
from jax import lax
from jax.experimental import pallas as pl
from jax.experimental.pallas import tpu as pltpu
from jax.sharding import PartitionSpec as P

ROW_RATE = 0.25
REL_RATE = 0.5
NEG_WEIGHT = 0.0625
F32 = jnp.float32
BF16 = jnp.bfloat16
NN = (((1,), (0,)), ((), ()))
NT = (((1,), (1,)), ((), ()))
TN = (((0,), (0,)), ((), ()))
VMEM = pl.BlockSpec(memory_space=pltpu.VMEM)
HBM = pl.BlockSpec(memory_space=pltpu.HBM)


def swapped(array, axis, stride):
    return lax.ppermute(array, axis, [(i, i ^ 1 << stride) for i in range(lax.axis_size(axis))])


def passed_along(array, axis, by):
    count = lax.axis_size(axis)
    return lax.ppermute(array, axis, [(i, (i + by) % count) for i in range(count)])


def sent(array, flips):
    n_src, n_dst = lax.axis_size("src"), lax.axis_size("dst")
    pairs = []
    for u in range(n_src):
        for w in range(n_dst):
            src_flip, dst_flip = flips[u % 2]
            pairs.append((u * n_dst + w, (u ^ src_flip) * n_dst + (w ^ dst_flip)))
    return lax.ppermute(array, ("src", "dst"), pairs)


def core_swapped(array):
    return sent(array, ((1, 0), (1, 0)))


def digits(count, unit):
    steps = []
    while count > 1:
        radix = 4 if count % 4 == 0 else 2
        steps.append((radix, unit))
        count, unit = count // radix, unit * radix
    return steps


def exchanged_terms(array):
    steps = [(0, r, u) for r, u in digits(lax.axis_size("src") // 2, 2)]
    steps += [(1, r, u) for r, u in digits(lax.axis_size("dst"), 1)]
    terms = None
    for axis, radix, unit in steps:

        def flip(k):
            return (0, k * unit) if axis else (k * unit, 0)

        if terms is None:
            one = sent(array, (flip(1), flip(1)))
            array = array + core_swapped(array)
            if radix == 4:
                two = sent(array, (flip(2), flip(2)))
                three = sent(array, (flip(3), flip(3)))
                (late,) = call(add_kernel, [VMEM] * 2, [array.shape], 10**9, [two, three])
                terms = ((array, one + core_swapped(one)), (late,))
            else:
                terms = ((array,), (one + core_swapped(one),))
            continue
        array = tree_sum([tree_sum(pair) for pair in terms])
        if radix == 4:
            odd = sent(array, (flip(1), flip(3)))
            two = sent(array, (flip(2), flip(2)))
            terms = ((array, two), (odd, core_swapped(odd)))
        else:
            terms = ((array,), (sent(array, (flip(1), flip(1))),))
    return [term for pair in terms for term in pair]


def tree_sum(terms):
    terms = list(terms)
    while len(terms) > 1:
        terms = [a + b for a, b in zip(terms[::2], terms[1::2])]
    return terms[0]


def packed_shape(rels, features):
    whole, rest = divmod(features, 128)
    assert rest * rels <= 8 * 128 and rels % 8 == 0
    return (whole * rels + (8 if rest else 0), 128)


def pack(out, values):
    rels, features = values.shape
    whole, rest = divmod(features, 128)
    for k in range(whole):
        out[k * rels : (k + 1) * rels, :] = values[:, k * 128 : (k + 1) * 128]
    if rest:
        tail = [values[8 * k : 8 * (k + 1), whole * 128 :] for k in range(rels // 8)]
        tail.append(jnp.zeros((8, 128 - rest * len(tail)), F32))
        out[whole * rels :, :] = jnp.concatenate(tail, axis=1)


def unpack(packed, rels, features):
    whole, rest = divmod(features, 128)
    parts = [packed[k * rels : (k + 1) * rels, :] for k in range(whole)]
    if rest:
        tail = packed[whole * rels :, :]
        tails = [tail[:, k * rest : (k + 1) * rest] for k in range(rels // 8)]
        parts.append(jnp.concatenate(tails, axis=0))
    return jnp.concatenate(parts, axis=1)


def halves(x):
    high = x.astype(BF16)
    return high, (x - high.astype(F32)).astype(BF16)


def dot(a, b, dims):
    return lax.dot_general(a, b, dims, preferred_element_type=F32)


def stacked(parts, dims, side):
    return jnp.concatenate(parts, axis=dims[0][side][0])


def dot_split(a, b, dims):
    if a[0].shape[dims[0][0][0]] % 128:
        return dot(a[0], b[0], dims) + dot(a[0], b[1], dims) + dot(a[1], b[0], dims)
    left = stacked((a[0], a[0], a[1]), dims, 0)
    return dot(left, stacked((b[0], b[1], b[0]), dims, 1), dims)


def dot_left(a, b, dims):
    if a[0].shape[dims[0][0][0]] % 128:
        return dot(a[0], b, dims) + dot(a[1], b, dims)
    return dot(stacked(a, dims, 0), stacked((b, b), dims, 1), dims)


def dot_right(a, b, dims):
    if b[0].shape[dims[0][1][0]] % 128:
        return dot(a, b[0], dims) + dot(a, b[1], dims)
    return dot(stacked((a, a), dims, 0), stacked(b, dims, 1), dims)


def onehot(index, length):
    return index == lax.broadcasted_iota(jnp.int32, (length, index.shape[1]), 0)


def as_bf16(mask):
    return jnp.where(mask, 1.0, 0.0).astype(BF16)


def negative_weight(negatives, rows, edges):
    ones = jnp.ones((negatives.shape[1], edges), BF16)
    return NEG_WEIGHT * dot(as_bf16(onehot(negatives, rows)), ones, NN)


def coefficient_parts(round_id, columns, edge_rows, counts, negatives):
    edges = edge_rows.shape[2]
    weight = negative_weight(negatives[round_id : round_id + 1, :], columns, edges)
    valid = lax.broadcasted_iota(jnp.int32, (1, edges), 1) < counts[:, round_id : round_id + 1]
    hit = jnp.where(onehot(edge_rows[round_id, 1:2, :], columns), 1.0, 0.0)
    scale = jnp.where(valid, 0.5 * (weight + hit), 0.0)
    return scale, scale - jnp.where(valid, hit, 0.0)


def coefficients(query, table_rows, scale, base):
    return scale * jnp.tanh(0.5 * dot_split(table_rows, query, NN)) + base


def row_step(table, state, gradient):
    new_state = state + jnp.sum(gradient * gradient, axis=0, keepdims=True) * (1.0 / table.shape[0])
    return table - gradient * (ROW_RATE / jnp.sqrt(new_state)), new_state


def hot_relations(round_id, edge_rel, rels):
    return as_bf16(onehot(edge_rel[round_id : round_id + 1, :], rels))


def first_front_kernel(
    src_hbm, state_hbm, dst_hbm, rel_hbm, rows_hbm, rels_hbm, counts_hbm, negs_hbm,
    top_out, bottom_out, query_out, coef_out, product_out,
    src, src_state, dst, rel, rows, rels, counts, negs, sems,
):
    features, columns = src.shape
    small = [
        (rows_hbm, rows), (rels_hbm, rels), (rel_hbm, rel), (counts_hbm, counts), (negs_hbm, negs),
    ]
    slabs = [(dst_hbm, dst), (src_hbm, src)]
    pairs = small + slabs + [(state_hbm, src_state)]
    copies = [pltpu.make_async_copy(a, b, sems.at[i]) for i, (a, b) in enumerate(pairs)]
    for copy in copies[len(small) :] + copies[: len(small)]:
        copy.start()
    for_dst, for_src, for_state = copies[len(small) :]
    for copy in copies[: len(small)]:
        copy.wait()
    src_hot = as_bf16(onehot(rows[0, 0:1, :], columns))
    rel_cols = dot_left(halves(rel[...]), hot_relations(0, rels, rel.shape[0]), TN)
    scale, base = coefficient_parts(0, columns, rows, counts, negs)
    for_dst.wait()
    table_dst = halves(dst[...])
    table_rows = halves(dst[...].T)
    for_src.wait()
    src_cols = dot_left(halves(src[...]), src_hot, NN)
    query = src_cols * rel_cols
    coef = coefficients(halves(query), table_rows, scale, base)
    query_grad = dot_split(table_dst, halves(coef), NN)
    src_grad = dot_left(halves(query_grad * rel_cols), src_hot, NT)
    for_state.wait()
    table, state = row_step(src[...], src_state[...], src_grad)
    top, rest = top_out.shape[0], features - top_out.shape[0]
    top_out[...] = table[0:top, :]
    bottom_out[0:rest, :] = table[top:, :]
    bottom_out[rest:, :] = jnp.broadcast_to(state, (bottom_out.shape[0] - rest, columns))
    query_out[...] = query
    coef_out[...] = coef
    product_out[...] = query_grad * src_cols


def first_back_kernel(
    dst, dst_state, query, coef, product, rel, rows, rels, counts, negs,
    spare_state, table_out, state_out, rel_first_out, rel_cols_out, scale_out, base_out, spare_out,
):
    grad = dot_split(halves(query[...]), halves(coef[...]), NT)
    table_out[...], state_out[...] = row_step(dst[...], dst_state[...], grad)
    rel_first_out[...] = dot_right(
        hot_relations(0, rels, rel.shape[0]), halves(product[...]), NT
    )
    rel_cols_out[...] = dot_left(halves(rel[...]), hot_relations(1, rels, rel.shape[0]), TN)
    scale_out[...], base_out[...] = coefficient_parts(1, dst.shape[1], rows, counts, negs)
    spare_out[...] = spare_state[...]


def second_gather_kernel(top, bottom, rel_cols, rows, src_cols_out, high_out, low_out):
    half, features = top.shape[0], rel_cols.shape[0]
    src_hot = as_bf16(onehot(rows[1, 0:1, :], top.shape[1]))
    for low, high, values in ((0, half, top[...]), (half, features, bottom[0 : features - half, :])):
        src_cols = dot_left(halves(values), src_hot, NN)
        src_cols_out[low:high, :] = src_cols
    high_out[...], low_out[...] = halves(src_cols_out[...] * rel_cols[...])


def second_front_kernel(
    spare, src_cols, high, low, rel_cols, scale, base, rels, rel_first, state,
    coef_out, scaled_out, rel_out, state_out,
):
    rel_hot = hot_relations(1, rels, rel_first.shape[0])
    coef = coefficients((high[...], low[...]), halves(spare[...].T), scale[...], base[...])
    query_grad = dot_split(halves(spare[...]), halves(coef), NN)
    pack(rel_out, rel_first[...] + dot_right(rel_hot, halves(query_grad * src_cols[...]), NT))
    state_out[...] = state[...]
    coef_out[...] = coef
    scaled_out[...] = query_grad * rel_cols[...]


def second_back_kernel(
    top, bottom, spare, spare_state, rows, high, low, coef, scaled,
    src_out, src_acc, spare_out, spare_acc,
):
    rest = spare.shape[0] - top.shape[0]
    src_hot = as_bf16(onehot(rows[1, 0:1, :], spare.shape[1]))
    src_grad = dot_left(halves(scaled[...]), src_hot, NT)
    moved = jnp.concatenate([top[...], bottom[0:rest, :]], axis=0)
    src_out[...], src_acc[...] = row_step(moved, bottom[rest : rest + 1, :], src_grad)
    spare_grad = dot_split((high[...], low[...]), halves(coef[...]), NT)
    spare_out[...], spare_acc[...] = row_step(spare[...], spare_state[...], spare_grad)


def add_kernel(left, right, out):
    out[...] = left[...] + right[...]


def relation_kernel(rel, rel_state, *refs):
    terms, (rel_out, state_out) = refs[:-2], refs[-2:]
    total = unpack(tree_sum([term[...] for term in terms]), *rel.shape)
    state = rel_state[...] + total * total
    state_out[...] = state
    rel_out[...] = rel[...] - REL_RATE * total / jnp.sqrt(state)


def call(kernel, in_specs, outs, flops, args, scratch=()):
    shapes = [a if isinstance(a, jax.ShapeDtypeStruct) else jax.ShapeDtypeStruct(a, F32) for a in outs]
    return pl.pallas_call(
        kernel,
        in_specs=in_specs,
        out_specs=[VMEM] * len(outs),
        out_shape=shapes,
        scratch_shapes=list(scratch),
        compiler_params=pltpu.CompilerParams(vmem_limit_bytes=40 * 1024 * 1024),
        cost_estimate=pl.CostEstimate(
            flops=flops, bytes_accessed=sum(a.size * 4 for a in args), transcendentals=0
        ),
    )(*args)


def per_device(
    src_table,
    src_state,
    dst_table,
    dst_state,
    spare_table,
    spare_state,
    relations,
    rel_state,
    edge_rows,
    edge_rel,
    counts,
    negatives,
):
    features, rows = src_table.shape
    edges = edge_rows.shape[2]
    rels = relations.shape[1]
    work = 2 * features * rows * edges
    rel = relations.T
    live = counts.T
    spare_in = swapped(spare_table, "dst", 0)
    operands = [
        src_table, src_state.reshape(1, rows), dst_table, rel, edge_rows, edge_rel, live, negatives,
    ]
    half = features // 16 * 8
    top, bottom, query, coef, product = call(
        first_front_kernel,
        [HBM] * 8,
        [
            (half, rows), (features - half + 8, rows), (features, edges), (rows, edges),
            (features, edges),
        ],
        400 * work,
        [pltpu.with_memory_space_constraint(a, pltpu.HBM) for a in operands],
        [pltpu.VMEM(a.shape, a.dtype) for a in operands]
        + [pltpu.SemaphoreType.DMA((len(operands),))],
    )
    top, bottom = passed_along((top, bottom), "src", 1)
    dst_next, dst_acc, rel_first, rel_cols, scale, base, spare_acc = call(
        first_back_kernel,
        [VMEM] * 11,
        [
            (features, rows), (1, rows), (rels, features), (features, edges), (rows, edges),
            (rows, edges), (1, rows),
        ],
        3 * work,
        [
            dst_table, dst_state.reshape(1, rows), query, coef, product,
            rel, edge_rows, edge_rel, live, negatives, spare_state.reshape(1, rows),
        ],
    )
    spare_acc_in = swapped(spare_acc, "dst", 0)
    src_cols, high, low = call(
        second_gather_kernel,
        [VMEM] * 4,
        [(features, edges)] + [jax.ShapeDtypeStruct((features, edges), BF16)] * 2,
        2 * work,
        [top, bottom, rel_cols, edge_rows],
    )
    coef, scaled, rel_both, spare_acc_in = call(
        second_front_kernel,
        [VMEM] * 10,
        [(rows, edges), (features, edges), packed_shape(rels, features), (1, rows)],
        10 * work,
        [
            spare_in, src_cols, high, low, rel_cols, scale, base, edge_rel, rel_first,
            spare_acc_in,
        ],
    )
    src_out, src_state_out, spare_out, spare_state_out = call(
        second_back_kernel,
        [VMEM] * 9,
        [(features, rows), (1, rows), (features, rows), (1, rows)],
        5 * work,
        [top, bottom, spare_in, spare_acc_in, edge_rows, high, low, coef, scaled],
    )
    terms = exchanged_terms(rel_both)
    relations_out, rel_state_out = call(
        relation_kernel,
        [VMEM] * (2 + len(terms)),
        [(rels, features), (rels, features)],
        rels * features,
        [rel, rel_state.T, *terms],
    )
    return (
        src_out,
        src_state_out.reshape(rows),
        dst_next,
        dst_acc.reshape(rows),
        spare_out,
        spare_state_out.reshape(rows),
        relations_out.T,
        rel_state_out.T,
    )


def solution(mesh):
    in_specs = (
        P(None, ("src", "dst")),
        P(("src", "dst")),
        P(None, ("src", "dst")),
        P(("src", "dst")),
        P(None, ("src", "dst")),
        P(("src", "dst")),
        P(),
        P(),
        P(None, None, ("src", "dst")),
        P(None, ("src", "dst")),
        P(None, ("src", "dst")),
        P(None, ("src", "dst")),
    )
    out_specs = (
        P(None, ("src", "dst")),
        P(("src", "dst")),
        P(None, ("src", "dst")),
        P(("src", "dst")),
        P(None, ("src", "dst")),
        P(("src", "dst")),
        P(),
        P(),
    )
    return jax.shard_map(
        per_device, mesh=mesh, in_specs=in_specs, out_specs=out_specs, check_vma=False
    )
```

```python
import jax
import jax.numpy as jnp
from jax import lax
from jax.experimental import pallas as pl
from jax.experimental.pallas import tpu as pltpu
from jax.sharding import PartitionSpec as P

ROW_RATE = 0.25
REL_RATE = 0.5
NEG_WEIGHT = 0.0625
F32 = jnp.float32
BF16 = jnp.bfloat16
NN = (((1,), (0,)), ((), ()))
NT = (((1,), (1,)), ((), ()))
TN = (((0,), (0,)), ((), ()))
VMEM = pl.BlockSpec(memory_space=pltpu.VMEM)
HBM = pl.BlockSpec(memory_space=pltpu.HBM)


def swapped(array, axis, stride):
    return lax.ppermute(array, axis, [(i, i ^ 1 << stride) for i in range(lax.axis_size(axis))])


def passed_along(array, axis, by):
    count = lax.axis_size(axis)
    return lax.ppermute(array, axis, [(i, (i + by) % count) for i in range(count)])


def sent(array, flips):
    n_src, n_dst = lax.axis_size("src"), lax.axis_size("dst")
    pairs = []
    for u in range(n_src):
        for w in range(n_dst):
            src_flip, dst_flip = flips[u % 2]
            pairs.append((u * n_dst + w, (u ^ src_flip) * n_dst + (w ^ dst_flip)))
    return lax.ppermute(array, ("src", "dst"), pairs)


def core_swapped(array):
    return sent(array, ((1, 0), (1, 0)))


def digits(count, unit):
    steps = []
    while count > 1:
        radix = 4 if count % 4 == 0 else 2
        steps.append((radix, unit))
        count, unit = count // radix, unit * radix
    return steps


def exchanged_terms(array):
    steps = [(0, r, u) for r, u in digits(lax.axis_size("src") // 2, 2)]
    steps += [(1, r, u) for r, u in digits(lax.axis_size("dst"), 1)]
    terms = None
    for axis, radix, unit in steps:

        def flip(k):
            return (0, k * unit) if axis else (k * unit, 0)

        if terms is None:
            one = sent(array, (flip(1), flip(1)))
            array = array + core_swapped(array)
            if radix == 4:
                two = sent(array, (flip(2), flip(2)))
                three = sent(array, (flip(3), flip(3)))
                (late,) = call(add_kernel, [VMEM] * 2, [array.shape], 10**9, [two, three])
                terms = ((array, one + core_swapped(one)), (late,))
            else:
                terms = ((array,), (one + core_swapped(one),))
            continue
        array = tree_sum([tree_sum(pair) for pair in terms])
        if radix == 4:
            odd = sent(array, (flip(1), flip(3)))
            two = sent(array, (flip(2), flip(2)))
            terms = ((array, two), (odd, core_swapped(odd)))
        else:
            terms = ((array,), (sent(array, (flip(1), flip(1))),))
    return [term for pair in terms for term in pair]


def tree_sum(terms):
    terms = list(terms)
    while len(terms) > 1:
        terms = [a + b for a, b in zip(terms[::2], terms[1::2])]
    return terms[0]


def packed_shape(rels, features):
    whole, rest = divmod(features, 128)
    assert rest * rels <= 8 * 128 and rels % 8 == 0
    return (whole * rels + (8 if rest else 0), 128)


def pack(out, values):
    rels, features = values.shape
    whole, rest = divmod(features, 128)
    for k in range(whole):
        out[k * rels : (k + 1) * rels, :] = values[:, k * 128 : (k + 1) * 128]
    if rest:
        tail = [values[8 * k : 8 * (k + 1), whole * 128 :] for k in range(rels // 8)]
        tail.append(jnp.zeros((8, 128 - rest * len(tail)), F32))
        out[whole * rels :, :] = jnp.concatenate(tail, axis=1)


def unpack(packed, rels, features):
    whole, rest = divmod(features, 128)
    parts = [packed[k * rels : (k + 1) * rels, :] for k in range(whole)]
    if rest:
        tail = packed[whole * rels :, :]
        tails = [tail[:, k * rest : (k + 1) * rest] for k in range(rels // 8)]
        parts.append(jnp.concatenate(tails, axis=0))
    return jnp.concatenate(parts, axis=1)


def halves(x):
    high = x.astype(BF16)
    return high, (x - high.astype(F32)).astype(BF16)


def dot(a, b, dims):
    return lax.dot_general(a, b, dims, preferred_element_type=F32)


def stacked(parts, dims, side):
    return jnp.concatenate(parts, axis=dims[0][side][0])


def dot_split(a, b, dims):
    if a[0].shape[dims[0][0][0]] % 128:
        return dot(a[0], b[0], dims) + dot(a[0], b[1], dims) + dot(a[1], b[0], dims)
    left = stacked((a[0], a[0], a[1]), dims, 0)
    return dot(left, stacked((b[0], b[1], b[0]), dims, 1), dims)


def dot_left(a, b, dims):
    if a[0].shape[dims[0][0][0]] % 128:
        return dot(a[0], b, dims) + dot(a[1], b, dims)
    return dot(stacked(a, dims, 0), stacked((b, b), dims, 1), dims)


def dot_right(a, b, dims):
    if b[0].shape[dims[0][1][0]] % 128:
        return dot(a, b[0], dims) + dot(a, b[1], dims)
    return dot(stacked((a, a), dims, 0), stacked(b, dims, 1), dims)


def onehot(index, length):
    return index == lax.broadcasted_iota(jnp.int32, (length, index.shape[1]), 0)


def as_bf16(mask):
    return jnp.where(mask, 1.0, 0.0).astype(BF16)


def negative_weight(negatives, rows, edges):
    ones = jnp.ones((negatives.shape[1], edges), BF16)
    return NEG_WEIGHT * dot(as_bf16(onehot(negatives, rows)), ones, NN)


def coefficient_parts(round_id, columns, edge_rows, counts, negatives):
    edges = edge_rows.shape[2]
    weight = negative_weight(negatives[round_id : round_id + 1, :], columns, edges)
    valid = lax.broadcasted_iota(jnp.int32, (1, edges), 1) < counts[:, round_id : round_id + 1]
    hit = jnp.where(onehot(edge_rows[round_id, 1:2, :], columns), 1.0, 0.0)
    scale = jnp.where(valid, 0.5 * (weight + hit), 0.0)
    return scale, scale - jnp.where(valid, hit, 0.0)


def coefficients(query, table_rows, scale, base):
    return scale * jnp.tanh(0.5 * dot_split(table_rows, query, NN)) + base


def row_step(table, state, gradient):
    new_state = state + jnp.sum(gradient * gradient, axis=0, keepdims=True) * (1.0 / table.shape[0])
    return table - gradient * (ROW_RATE / jnp.sqrt(new_state)), new_state


def hot_relations(round_id, edge_rel, rels):
    return as_bf16(onehot(edge_rel[round_id : round_id + 1, :], rels))


def first_front_kernel(
    src_hbm, state_hbm, dst_hbm, rel_hbm, rows_hbm, rels_hbm, counts_hbm, negs_hbm,
    top_out, bottom_out, query_out, coef_out, product_out,
    src, src_state, dst, rel, rows, rels, counts, negs, sems,
):
    features, columns = src.shape
    small = [
        (rows_hbm, rows), (rels_hbm, rels), (rel_hbm, rel), (counts_hbm, counts), (negs_hbm, negs),
    ]
    slabs = [(dst_hbm, dst), (src_hbm, src)]
    pairs = small + slabs + [(state_hbm, src_state)]
    copies = [pltpu.make_async_copy(a, b, sems.at[i]) for i, (a, b) in enumerate(pairs)]
    for copy in copies:
        copy.start()
    for_dst, for_src, for_state = copies[len(small) :]
    for copy in copies[: len(small)]:
        copy.wait()
    src_hot = as_bf16(onehot(rows[0, 0:1, :], columns))
    rel_cols = dot_left(halves(rel[...]), hot_relations(0, rels, rel.shape[0]), TN)
    for_dst.wait()
    for_src.wait()
    table_dst = halves(dst[...])
    table_rows = halves(dst[...].T)
    src_cols = dot_left(halves(src[...]), src_hot, NN)
    query = src_cols * rel_cols
    scale, base = coefficient_parts(0, columns, rows, counts, negs)
    coef = coefficients(halves(query), table_rows, scale, base)
    query_grad = dot_split(table_dst, halves(coef), NN)
    src_grad = dot_left(halves(query_grad * rel_cols), src_hot, NT)
    for_state.wait()
    table, state = row_step(src[...], src_state[...], src_grad)
    top, rest = top_out.shape[0], features - top_out.shape[0]
    top_out[...] = table[0:top, :]
    bottom_out[0:rest, :] = table[top:, :]
    bottom_out[rest:, :] = jnp.broadcast_to(state, (bottom_out.shape[0] - rest, columns))
    query_out[...] = query
    coef_out[...] = coef
    product_out[...] = query_grad * src_cols


def first_back_kernel(
    dst, dst_state, query, coef, product, rel, rows, rels, counts, negs,
    spare_state, table_out, state_out, rel_first_out, rel_cols_out, scale_out, base_out, spare_out,
):
    grad = dot_split(halves(query[...]), halves(coef[...]), NT)
    table_out[...], state_out[...] = row_step(dst[...], dst_state[...], grad)
    rel_first_out[...] = dot_right(
        hot_relations(0, rels, rel.shape[0]), halves(product[...]), NT
    )
    rel_cols_out[...] = dot_left(halves(rel[...]), hot_relations(1, rels, rel.shape[0]), TN)
    scale_out[...], base_out[...] = coefficient_parts(1, dst.shape[1], rows, counts, negs)
    spare_out[...] = spare_state[...]


def second_gather_kernel(top, bottom, rel_cols, rows, src_cols_out, high_out, low_out):
    half, features = top.shape[0], rel_cols.shape[0]
    src_hot = as_bf16(onehot(rows[1, 0:1, :], top.shape[1]))
    for low, high, values in ((0, half, top[...]), (half, features, bottom[0 : features - half, :])):
        src_cols = dot_left(halves(values), src_hot, NN)
        src_cols_out[low:high, :] = src_cols
    high_out[...], low_out[...] = halves(src_cols_out[...] * rel_cols[...])


def second_front_kernel(
    spare, src_cols, high, low, rel_cols, scale, base, rels, rel_first, state,
    coef_out, scaled_out, rel_out, state_out,
):
    rel_hot = hot_relations(1, rels, rel_first.shape[0])
    coef = coefficients((high[...], low[...]), halves(spare[...].T), scale[...], base[...])
    query_grad = dot_split(halves(spare[...]), halves(coef), NN)
    pack(rel_out, rel_first[...] + dot_right(rel_hot, halves(query_grad * src_cols[...]), NT))
    state_out[...] = state[...]
    coef_out[...] = coef
    scaled_out[...] = query_grad * rel_cols[...]


def second_back_kernel(
    top, bottom, spare, spare_state, rows, high, low, coef, scaled,
    src_out, src_acc, spare_out, spare_acc,
):
    rest = spare.shape[0] - top.shape[0]
    src_hot = as_bf16(onehot(rows[1, 0:1, :], spare.shape[1]))
    src_grad = dot_left(halves(scaled[...]), src_hot, NT)
    moved = jnp.concatenate([top[...], bottom[0:rest, :]], axis=0)
    src_out[...], src_acc[...] = row_step(moved, bottom[rest : rest + 1, :], src_grad)
    spare_grad = dot_split((high[...], low[...]), halves(coef[...]), NT)
    spare_out[...], spare_acc[...] = row_step(spare[...], spare_state[...], spare_grad)


def add_kernel(left, right, out):
    out[...] = left[...] + right[...]


def relation_kernel(rel, rel_state, *refs):
    terms, (rel_out, state_out) = refs[:-2], refs[-2:]
    total = unpack(tree_sum([term[...] for term in terms]), *rel.shape)
    state = rel_state[...] + total * total
    state_out[...] = state
    rel_out[...] = rel[...] - REL_RATE * total / jnp.sqrt(state)


def call(kernel, in_specs, outs, flops, args, scratch=()):
    shapes = [a if isinstance(a, jax.ShapeDtypeStruct) else jax.ShapeDtypeStruct(a, F32) for a in outs]
    return pl.pallas_call(
        kernel,
        in_specs=in_specs,
        out_specs=[VMEM] * len(outs),
        out_shape=shapes,
        scratch_shapes=list(scratch),
        compiler_params=pltpu.CompilerParams(vmem_limit_bytes=40 * 1024 * 1024),
        cost_estimate=pl.CostEstimate(
            flops=flops, bytes_accessed=sum(a.size * 4 for a in args), transcendentals=0
        ),
    )(*args)


def per_device(
    src_table,
    src_state,
    dst_table,
    dst_state,
    spare_table,
    spare_state,
    relations,
    rel_state,
    edge_rows,
    edge_rel,
    counts,
    negatives,
):
    features, rows = src_table.shape
    edges = edge_rows.shape[2]
    rels = relations.shape[1]
    work = 2 * features * rows * edges
    rel = relations.T
    live = counts.T
    spare_in = swapped(spare_table, "dst", 0)
    operands = [
        src_table, src_state.reshape(1, rows), dst_table, rel, edge_rows, edge_rel, live, negatives,
    ]
    half = features // 16 * 8
    top, bottom, query, coef, product = call(
        first_front_kernel,
        [HBM] * 8,
        [
            (half, rows), (features - half + 8, rows), (features, edges), (rows, edges),
            (features, edges),
        ],
        400 * work,
        [pltpu.with_memory_space_constraint(a, pltpu.HBM) for a in operands],
        [pltpu.VMEM(a.shape, a.dtype) for a in operands]
        + [pltpu.SemaphoreType.DMA((len(operands),))],
    )
    top, bottom = passed_along((top, bottom), "src", 1)
    dst_next, dst_acc, rel_first, rel_cols, scale, base, spare_acc = call(
        first_back_kernel,
        [VMEM] * 11,
        [
            (features, rows), (1, rows), (rels, features), (features, edges), (rows, edges),
            (rows, edges), (1, rows),
        ],
        3 * work,
        [
            dst_table, dst_state.reshape(1, rows), query, coef, product,
            rel, edge_rows, edge_rel, live, negatives, spare_state.reshape(1, rows),
        ],
    )
    spare_acc_in = swapped(spare_acc, "dst", 0)
    src_cols, high, low = call(
        second_gather_kernel,
        [VMEM] * 4,
        [(features, edges)] + [jax.ShapeDtypeStruct((features, edges), BF16)] * 2,
        2 * work,
        [top, bottom, rel_cols, edge_rows],
    )
    coef, scaled, rel_both, spare_acc_in = call(
        second_front_kernel,
        [VMEM] * 10,
        [(rows, edges), (features, edges), packed_shape(rels, features), (1, rows)],
        10 * work,
        [
            spare_in, src_cols, high, low, rel_cols, scale, base, edge_rel, rel_first,
            spare_acc_in,
        ],
    )
    src_out, src_state_out, spare_out, spare_state_out = call(
        second_back_kernel,
        [VMEM] * 9,
        [(features, rows), (1, rows), (features, rows), (1, rows)],
        5 * work,
        [top, bottom, spare_in, spare_acc_in, edge_rows, high, low, coef, scaled],
    )
    terms = exchanged_terms(rel_both)
    relations_out, rel_state_out = call(
        relation_kernel,
        [VMEM] * (2 + len(terms)),
        [(rels, features), (rels, features)],
        rels * features,
        [rel, rel_state.T, *terms],
    )
    return (
        src_out,
        src_state_out.reshape(rows),
        dst_next,
        dst_acc.reshape(rows),
        spare_out,
        spare_state_out.reshape(rows),
        relations_out.T,
        rel_state_out.T,
    )


def solution(mesh):
    in_specs = (
        P(None, ("src", "dst")),
        P(("src", "dst")),
        P(None, ("src", "dst")),
        P(("src", "dst")),
        P(None, ("src", "dst")),
        P(("src", "dst")),
        P(),
        P(),
        P(None, None, ("src", "dst")),
        P(None, ("src", "dst")),
        P(None, ("src", "dst")),
        P(None, ("src", "dst")),
    )
    out_specs = (
        P(None, ("src", "dst")),
        P(("src", "dst")),
        P(None, ("src", "dst")),
        P(("src", "dst")),
        P(None, ("src", "dst")),
        P(("src", "dst")),
        P(),
        P(),
    )
    return jax.shard_map(
        per_device, mesh=mesh, in_specs=in_specs, out_specs=out_specs, check_vma=False
    )
```

```python
import jax
import jax.numpy as jnp
from jax import lax
from jax.experimental import pallas as pl
from jax.experimental.pallas import tpu as pltpu
from jax.sharding import PartitionSpec as P

ROW_RATE = 0.25
REL_RATE = 0.5
NEG_WEIGHT = 0.0625
F32 = jnp.float32
BF16 = jnp.bfloat16
NN = (((1,), (0,)), ((), ()))
NT = (((1,), (1,)), ((), ()))
TN = (((0,), (0,)), ((), ()))
VMEM = pl.BlockSpec(memory_space=pltpu.VMEM)
HBM = pl.BlockSpec(memory_space=pltpu.HBM)


def swapped(array, axis, stride):
    return lax.ppermute(array, axis, [(i, i ^ 1 << stride) for i in range(lax.axis_size(axis))])


def passed_along(array, axis, by):
    count = lax.axis_size(axis)
    return lax.ppermute(array, axis, [(i, (i + by) % count) for i in range(count)])


def sent(array, flips):
    n_src, n_dst = lax.axis_size("src"), lax.axis_size("dst")
    pairs = []
    for u in range(n_src):
        for w in range(n_dst):
            src_flip, dst_flip = flips[u % 2]
            pairs.append((u * n_dst + w, (u ^ src_flip) * n_dst + (w ^ dst_flip)))
    return lax.ppermute(array, ("src", "dst"), pairs)


def core_swapped(array):
    return sent(array, ((1, 0), (1, 0)))


def digits(count, unit):
    steps = []
    while count > 1:
        radix = 4 if count % 4 == 0 else 2
        steps.append((radix, unit))
        count, unit = count // radix, unit * radix
    return steps


def exchanged_terms(array):
    steps = [(0, r, u) for r, u in digits(lax.axis_size("src") // 2, 2)]
    steps += [(1, r, u) for r, u in digits(lax.axis_size("dst"), 1)]
    terms = None
    for axis, radix, unit in steps:

        def flip(k):
            return (0, k * unit) if axis else (k * unit, 0)

        if terms is None:
            one = sent(array, (flip(1), flip(1)))
            array = array + core_swapped(array)
            if radix == 4:
                rest = sent(array, (flip(2), flip(3)))
                terms = ((array, one + core_swapped(one)), (rest, core_swapped(rest)))
            else:
                terms = ((array,), (one + core_swapped(one),))
            continue
        array = tree_sum([tree_sum(pair) for pair in terms])
        if radix == 4:
            odd = sent(array, (flip(1), flip(3)))
            two = sent(array, (flip(2), flip(2)))
            terms = ((array, two), (odd, core_swapped(odd)))
        else:
            terms = ((array,), (sent(array, (flip(1), flip(1))),))
    return [term for pair in terms for term in pair]


def tree_sum(terms):
    terms = list(terms)
    while len(terms) > 1:
        terms = [a + b for a, b in zip(terms[::2], terms[1::2])]
    return terms[0]


def packed_shape(rels, features):
    whole, rest = divmod(features, 128)
    assert rest * rels <= 8 * 128 and rels % 8 == 0
    return (whole * rels + (8 if rest else 0), 128)


def pack(out, values):
    rels, features = values.shape
    whole, rest = divmod(features, 128)
    for k in range(whole):
        out[k * rels : (k + 1) * rels, :] = values[:, k * 128 : (k + 1) * 128]
    if rest:
        tail = [values[8 * k : 8 * (k + 1), whole * 128 :] for k in range(rels // 8)]
        tail.append(jnp.zeros((8, 128 - rest * len(tail)), F32))
        out[whole * rels :, :] = jnp.concatenate(tail, axis=1)


def unpack(packed, rels, features):
    whole, rest = divmod(features, 128)
    parts = [packed[k * rels : (k + 1) * rels, :] for k in range(whole)]
    if rest:
        tail = packed[whole * rels :, :]
        tails = [tail[:, k * rest : (k + 1) * rest] for k in range(rels // 8)]
        parts.append(jnp.concatenate(tails, axis=0))
    return jnp.concatenate(parts, axis=1)


def halves(x):
    high = x.astype(BF16)
    return high, (x - high.astype(F32)).astype(BF16)


def dot(a, b, dims):
    return lax.dot_general(a, b, dims, preferred_element_type=F32)


def stacked(parts, dims, side):
    return jnp.concatenate(parts, axis=dims[0][side][0])


def dot_split(a, b, dims):
    if a[0].shape[dims[0][0][0]] % 128:
        return dot(a[0], b[0], dims) + dot(a[0], b[1], dims) + dot(a[1], b[0], dims)
    left = stacked((a[0], a[0], a[1]), dims, 0)
    return dot(left, stacked((b[0], b[1], b[0]), dims, 1), dims)


def dot_left(a, b, dims):
    if a[0].shape[dims[0][0][0]] % 128:
        return dot(a[0], b, dims) + dot(a[1], b, dims)
    return dot(stacked(a, dims, 0), stacked((b, b), dims, 1), dims)


def dot_right(a, b, dims):
    if b[0].shape[dims[0][1][0]] % 128:
        return dot(a, b[0], dims) + dot(a, b[1], dims)
    return dot(stacked((a, a), dims, 0), stacked(b, dims, 1), dims)


def onehot(index, length):
    return index == lax.broadcasted_iota(jnp.int32, (length, index.shape[1]), 0)


def as_bf16(mask):
    return jnp.where(mask, 1.0, 0.0).astype(BF16)


def negative_weight(negatives, rows, edges):
    ones = jnp.ones((negatives.shape[1], edges), BF16)
    return NEG_WEIGHT * dot(as_bf16(onehot(negatives, rows)), ones, NN)


def coefficient_parts(round_id, columns, edge_rows, counts, negatives):
    edges = edge_rows.shape[2]
    weight = negative_weight(negatives[round_id : round_id + 1, :], columns, edges)
    valid = lax.broadcasted_iota(jnp.int32, (1, edges), 1) < counts[:, round_id : round_id + 1]
    hit = jnp.where(onehot(edge_rows[round_id, 1:2, :], columns), 1.0, 0.0)
    scale = jnp.where(valid, 0.5 * (weight + hit), 0.0)
    return scale, scale - jnp.where(valid, hit, 0.0)


def coefficients(query, table_rows, scale, base):
    return scale * jnp.tanh(0.5 * dot_split(table_rows, query, NN)) + base


def row_step(table, state, gradient):
    new_state = state + jnp.sum(gradient * gradient, axis=0, keepdims=True) * (1.0 / table.shape[0])
    return table - gradient * (ROW_RATE / jnp.sqrt(new_state)), new_state


def hot_relations(round_id, edge_rel, rels):
    return as_bf16(onehot(edge_rel[round_id : round_id + 1, :], rels))


def first_front_kernel(
    src_hbm, state_hbm, dst_hbm, rel_hbm, rows_hbm, rels_hbm, counts_hbm, negs_hbm,
    top_out, bottom_out, query_out, coef_out, product_out,
    src, src_state, dst, rel, rows, rels, counts, negs, sems,
):
    features, columns = src.shape
    small = [
        (rows_hbm, rows), (rels_hbm, rels), (rel_hbm, rel), (counts_hbm, counts), (negs_hbm, negs),
    ]
    slabs = [(dst_hbm, dst), (src_hbm, src)]
    pairs = small + slabs + [(state_hbm, src_state)]
    copies = [pltpu.make_async_copy(a, b, sems.at[i]) for i, (a, b) in enumerate(pairs)]
    for copy in copies:
        copy.start()
    for_dst, for_src, for_state = copies[len(small) :]
    for copy in copies[: len(small)]:
        copy.wait()
    src_hot = as_bf16(onehot(rows[0, 0:1, :], columns))
    rel_cols = dot_left(halves(rel[...]), hot_relations(0, rels, rel.shape[0]), TN)
    for_dst.wait()
    for_src.wait()
    table_dst = halves(dst[...])
    table_rows = halves(dst[...].T)
    src_cols = dot_left(halves(src[...]), src_hot, NN)
    query = src_cols * rel_cols
    scale, base = coefficient_parts(0, columns, rows, counts, negs)
    coef = coefficients(halves(query), table_rows, scale, base)
    query_grad = dot_split(table_dst, halves(coef), NN)
    src_grad = dot_left(halves(query_grad * rel_cols), src_hot, NT)
    for_state.wait()
    table, state = row_step(src[...], src_state[...], src_grad)
    top, rest = top_out.shape[0], features - top_out.shape[0]
    top_out[...] = table[0:top, :]
    bottom_out[0:rest, :] = table[top:, :]
    bottom_out[rest:, :] = jnp.broadcast_to(state, (bottom_out.shape[0] - rest, columns))
    query_out[...] = query
    coef_out[...] = coef
    product_out[...] = query_grad * src_cols


def first_back_kernel(
    dst, dst_state, query, coef, product, rel, rows, rels, counts, negs,
    spare_state, table_out, state_out, rel_first_out, rel_cols_out, scale_out, base_out, spare_out,
):
    grad = dot_split(halves(query[...]), halves(coef[...]), NT)
    table_out[...], state_out[...] = row_step(dst[...], dst_state[...], grad)
    rel_first_out[...] = dot_right(
        hot_relations(0, rels, rel.shape[0]), halves(product[...]), NT
    )
    rel_cols_out[...] = dot_left(halves(rel[...]), hot_relations(1, rels, rel.shape[0]), TN)
    scale_out[...], base_out[...] = coefficient_parts(1, dst.shape[1], rows, counts, negs)
    spare_out[...] = spare_state[...]


def second_gather_kernel(top, bottom, rel_cols, rows, src_cols_out, high_out, low_out):
    half, features = top.shape[0], rel_cols.shape[0]
    src_hot = as_bf16(onehot(rows[1, 0:1, :], top.shape[1]))
    for low, high, values in ((0, half, top[...]), (half, features, bottom[0 : features - half, :])):
        src_cols = dot_left(halves(values), src_hot, NN)
        src_cols_out[low:high, :] = src_cols
    high_out[...], low_out[...] = halves(src_cols_out[...] * rel_cols[...])


def second_front_kernel(
    spare, src_cols, high, low, rel_cols, scale, base, rels, rel_first, state,
    coef_out, scaled_out, rel_out, state_out,
):
    rel_hot = hot_relations(1, rels, rel_first.shape[0])
    coef = coefficients((high[...], low[...]), halves(spare[...].T), scale[...], base[...])
    query_grad = dot_split(halves(spare[...]), halves(coef), NN)
    pack(rel_out, rel_first[...] + dot_right(rel_hot, halves(query_grad * src_cols[...]), NT))
    state_out[...] = state[...]
    coef_out[...] = coef
    scaled_out[...] = query_grad * rel_cols[...]


def second_back_kernel(
    top, bottom, spare, spare_state, rows, high, low, coef, scaled,
    src_out, src_acc, spare_out, spare_acc,
):
    rest = spare.shape[0] - top.shape[0]
    src_hot = as_bf16(onehot(rows[1, 0:1, :], spare.shape[1]))
    src_grad = dot_left(halves(scaled[...]), src_hot, NT)
    moved = jnp.concatenate([top[...], bottom[0:rest, :]], axis=0)
    src_out[...], src_acc[...] = row_step(moved, bottom[rest : rest + 1, :], src_grad)
    spare_grad = dot_split((high[...], low[...]), halves(coef[...]), NT)
    spare_out[...], spare_acc[...] = row_step(spare[...], spare_state[...], spare_grad)


def relation_kernel(rel, rel_state, *refs):
    terms, (rel_out, state_out) = refs[:-2], refs[-2:]
    total = unpack(tree_sum([term[...] for term in terms]), *rel.shape)
    state = rel_state[...] + total * total
    state_out[...] = state
    rel_out[...] = rel[...] - REL_RATE * total / jnp.sqrt(state)


def call(kernel, in_specs, outs, flops, args, scratch=()):
    shapes = [a if isinstance(a, jax.ShapeDtypeStruct) else jax.ShapeDtypeStruct(a, F32) for a in outs]
    return pl.pallas_call(
        kernel,
        in_specs=in_specs,
        out_specs=[VMEM] * len(outs),
        out_shape=shapes,
        scratch_shapes=list(scratch),
        compiler_params=pltpu.CompilerParams(vmem_limit_bytes=40 * 1024 * 1024),
        cost_estimate=pl.CostEstimate(
            flops=flops, bytes_accessed=sum(a.size * 4 for a in args), transcendentals=0
        ),
    )(*args)


def per_device(
    src_table,
    src_state,
    dst_table,
    dst_state,
    spare_table,
    spare_state,
    relations,
    rel_state,
    edge_rows,
    edge_rel,
    counts,
    negatives,
):
    features, rows = src_table.shape
    edges = edge_rows.shape[2]
    rels = relations.shape[1]
    work = 2 * features * rows * edges
    rel = relations.T
    live = counts.T
    spare_in = swapped(spare_table, "dst", 0)
    operands = [
        src_table, src_state.reshape(1, rows), dst_table, rel, edge_rows, edge_rel, live, negatives,
    ]
    half = features // 16 * 8
    top, bottom, query, coef, product = call(
        first_front_kernel,
        [HBM] * 8,
        [
            (half, rows), (features - half + 8, rows), (features, edges), (rows, edges),
            (features, edges),
        ],
        400 * work,
        [pltpu.with_memory_space_constraint(a, pltpu.HBM) for a in operands],
        [pltpu.VMEM(a.shape, a.dtype) for a in operands]
        + [pltpu.SemaphoreType.DMA((len(operands),))],
    )
    top, bottom = passed_along((top, bottom), "src", 1)
    dst_next, dst_acc, rel_first, rel_cols, scale, base, spare_acc = call(
        first_back_kernel,
        [VMEM] * 11,
        [
            (features, rows), (1, rows), (rels, features), (features, edges), (rows, edges),
            (rows, edges), (1, rows),
        ],
        3 * work,
        [
            dst_table, dst_state.reshape(1, rows), query, coef, product,
            rel, edge_rows, edge_rel, live, negatives, spare_state.reshape(1, rows),
        ],
    )
    spare_acc_in = swapped(spare_acc, "dst", 0)
    src_cols, high, low = call(
        second_gather_kernel,
        [VMEM] * 4,
        [(features, edges)] + [jax.ShapeDtypeStruct((features, edges), BF16)] * 2,
        2 * work,
        [top, bottom, rel_cols, edge_rows],
    )
    coef, scaled, rel_both, spare_acc_in = call(
        second_front_kernel,
        [VMEM] * 10,
        [(rows, edges), (features, edges), packed_shape(rels, features), (1, rows)],
        10 * work,
        [
            spare_in, src_cols, high, low, rel_cols, scale, base, edge_rel, rel_first,
            spare_acc_in,
        ],
    )
    src_out, src_state_out, spare_out, spare_state_out = call(
        second_back_kernel,
        [VMEM] * 9,
        [(features, rows), (1, rows), (features, rows), (1, rows)],
        5 * work,
        [top, bottom, spare_in, spare_acc_in, edge_rows, high, low, coef, scaled],
    )
    terms = exchanged_terms(rel_both)
    relations_out, rel_state_out = call(
        relation_kernel,
        [VMEM] * (2 + len(terms)),
        [(rels, features), (rels, features)],
        rels * features,
        [rel, rel_state.T, *terms],
    )
    return (
        src_out,
        src_state_out.reshape(rows),
        dst_next,
        dst_acc.reshape(rows),
        spare_out,
        spare_state_out.reshape(rows),
        relations_out.T,
        rel_state_out.T,
    )


def solution(mesh):
    in_specs = (
        P(None, ("src", "dst")),
        P(("src", "dst")),
        P(None, ("src", "dst")),
        P(("src", "dst")),
        P(None, ("src", "dst")),
        P(("src", "dst")),
        P(),
        P(),
        P(None, None, ("src", "dst")),
        P(None, ("src", "dst")),
        P(None, ("src", "dst")),
        P(None, ("src", "dst")),
    )
    out_specs = (
        P(None, ("src", "dst")),
        P(("src", "dst")),
        P(None, ("src", "dst")),
        P(("src", "dst")),
        P(None, ("src", "dst")),
        P(("src", "dst")),
        P(),
        P(),
    )
    return jax.shard_map(
        per_device, mesh=mesh, in_specs=in_specs, out_specs=out_specs, check_vma=False
    )
```

```python
import jax
import jax.numpy as jnp
from jax import lax
from jax.experimental import pallas as pl
from jax.experimental.pallas import tpu as pltpu
from jax.sharding import PartitionSpec as P

ROW_RATE = 0.25
REL_RATE = 0.5
NEG_WEIGHT = 0.0625
F32 = jnp.float32
BF16 = jnp.bfloat16
NN = (((1,), (0,)), ((), ()))
NT = (((1,), (1,)), ((), ()))
TN = (((0,), (0,)), ((), ()))
VMEM = pl.BlockSpec(memory_space=pltpu.VMEM)
HBM = pl.BlockSpec(memory_space=pltpu.HBM)


def swapped(array, axis, stride):
    return lax.ppermute(array, axis, [(i, i ^ 1 << stride) for i in range(lax.axis_size(axis))])


def passed_along(array, axis, by):
    count = lax.axis_size(axis)
    return lax.ppermute(array, axis, [(i, (i + by) % count) for i in range(count)])


def sent(array, flips):
    n_src, n_dst = lax.axis_size("src"), lax.axis_size("dst")
    pairs = []
    for u in range(n_src):
        for w in range(n_dst):
            src_flip, dst_flip = flips[u % 2]
            pairs.append((u * n_dst + w, (u ^ src_flip) * n_dst + (w ^ dst_flip)))
    return lax.ppermute(array, ("src", "dst"), pairs)


def core_swapped(array):
    return sent(array, ((1, 0), (1, 0)))


def digits(count, unit):
    steps = []
    while count > 1:
        radix = 4 if count % 4 == 0 else 2
        steps.append((radix, unit))
        count, unit = count // radix, unit * radix
    return steps


def exchanged_terms(array):
    steps = [(0, r, u) for r, u in digits(lax.axis_size("src") // 2, 2)]
    steps += [(1, r, u) for r, u in digits(lax.axis_size("dst"), 1)]
    terms = None
    for axis, radix, unit in steps:

        def flip(k):
            return (0, k * unit) if axis else (k * unit, 0)

        if terms is None:
            one = sent(array, (flip(1), flip(1)))
            array = array + core_swapped(array)
            if radix == 4:
                two = sent(array, (flip(2), flip(2)))
                three = sent(array, (flip(3), flip(3)))
                (late,) = call(add_kernel, [VMEM] * 2, [array.shape], 10**9, [two, three])
                terms = ((array, one + core_swapped(one)), (late,))
            else:
                terms = ((array,), (one + core_swapped(one),))
            continue
        array = tree_sum([tree_sum(pair) for pair in terms])
        if radix == 4:
            odd = sent(array, (flip(1), flip(3)))
            two = sent(array, (flip(2), flip(2)))
            terms = ((array, two), (odd, core_swapped(odd)))
        else:
            terms = ((array,), (sent(array, (flip(1), flip(1))),))
    return [term for pair in terms for term in pair]


def tree_sum(terms):
    terms = list(terms)
    while len(terms) > 1:
        terms = [a + b for a, b in zip(terms[::2], terms[1::2])]
    return terms[0]


def packed_shape(rels, features):
    whole, rest = divmod(features, 128)
    assert rest * rels <= 8 * 128 and rels % 8 == 0
    return (whole * rels + (8 if rest else 0), 128)


def pack(out, values):
    rels, features = values.shape
    whole, rest = divmod(features, 128)
    for k in range(whole):
        out[k * rels : (k + 1) * rels, :] = values[:, k * 128 : (k + 1) * 128]
    if rest:
        tail = [values[8 * k : 8 * (k + 1), whole * 128 :] for k in range(rels // 8)]
        tail.append(jnp.zeros((8, 128 - rest * len(tail)), F32))
        out[whole * rels :, :] = jnp.concatenate(tail, axis=1)


def unpack(packed, rels, features):
    whole, rest = divmod(features, 128)
    parts = [packed[k * rels : (k + 1) * rels, :] for k in range(whole)]
    if rest:
        tail = packed[whole * rels :, :]
        tails = [tail[:, k * rest : (k + 1) * rest] for k in range(rels // 8)]
        parts.append(jnp.concatenate(tails, axis=0))
    return jnp.concatenate(parts, axis=1)


def halves(x):
    high = x.astype(BF16)
    return high, (x - high.astype(F32)).astype(BF16)


def dot(a, b, dims):
    return lax.dot_general(a, b, dims, preferred_element_type=F32)


def stacked(parts, dims, side):
    return jnp.concatenate(parts, axis=dims[0][side][0])


def dot_split(a, b, dims):
    if a[0].shape[dims[0][0][0]] % 128:
        return dot(a[0], b[0], dims) + dot(a[0], b[1], dims) + dot(a[1], b[0], dims)
    left = stacked((a[0], a[0], a[1]), dims, 0)
    return dot(left, stacked((b[0], b[1], b[0]), dims, 1), dims)


def dot_left(a, b, dims):
    if a[0].shape[dims[0][0][0]] % 128:
        return dot(a[0], b, dims) + dot(a[1], b, dims)
    return dot(stacked(a, dims, 0), stacked((b, b), dims, 1), dims)


def dot_right(a, b, dims):
    if b[0].shape[dims[0][1][0]] % 128:
        return dot(a, b[0], dims) + dot(a, b[1], dims)
    return dot(stacked((a, a), dims, 0), stacked(b, dims, 1), dims)


def onehot(index, length):
    return index == lax.broadcasted_iota(jnp.int32, (length, index.shape[1]), 0)


def as_bf16(mask):
    return jnp.where(mask, 1.0, 0.0).astype(BF16)


def negative_weight(negatives, rows, edges):
    ones = jnp.ones((negatives.shape[1], edges), BF16)
    return NEG_WEIGHT * dot(as_bf16(onehot(negatives, rows)), ones, NN)


def coefficient_parts(round_id, columns, edge_rows, counts, negatives):
    edges = edge_rows.shape[2]
    weight = negative_weight(negatives[round_id : round_id + 1, :], columns, edges)
    valid = lax.broadcasted_iota(jnp.int32, (1, edges), 1) < counts[:, round_id : round_id + 1]
    hit = jnp.where(onehot(edge_rows[round_id, 1:2, :], columns), 1.0, 0.0)
    scale = jnp.where(valid, 0.5 * (weight + hit), 0.0)
    return scale, scale - jnp.where(valid, hit, 0.0)


def coefficients(query, table_rows, scale, base):
    return scale * jnp.tanh(0.5 * dot_split(table_rows, query, NN)) + base


def row_step(table, state, gradient):
    new_state = state + jnp.sum(gradient * gradient, axis=0, keepdims=True) * (1.0 / table.shape[0])
    return table - gradient * (ROW_RATE * lax.rsqrt(new_state)), new_state


def hot_relations(round_id, edge_rel, rels):
    return as_bf16(onehot(edge_rel[round_id : round_id + 1, :], rels))


def first_front_kernel(
    src_hbm, state_hbm, dst_hbm, rel_hbm, rows_hbm, rels_hbm, counts_hbm, negs_hbm,
    top_out, bottom_out, query_out, coef_out, product_out,
    src, src_state, dst, rel, rows, rels, counts, negs, sems,
):
    features, columns = src.shape
    small = [
        (rows_hbm, rows), (rels_hbm, rels), (rel_hbm, rel), (counts_hbm, counts), (negs_hbm, negs),
    ]
    half = features // 32 * 16
    halves_of = [pl.ds(0, half), pl.ds(half, features - half)]
    slabs = [(whole.at[c], part.at[c]) for whole, part in ((dst_hbm, dst), (src_hbm, src)) for c in halves_of]
    pairs = small + slabs + [(state_hbm, src_state)]
    copies = [pltpu.make_async_copy(a, b, sems.at[i]) for i, (a, b) in enumerate(pairs)]
    for copy in copies:
        copy.start()
    *for_slabs, for_state = copies[len(small) :]
    for copy in copies[: len(small)]:
        copy.wait()
    src_hot = as_bf16(onehot(rows[0, 0:1, :], columns))
    rel_cols = dot_left(halves(rel[...]), hot_relations(0, rels, rel.shape[0]), TN)
    for copy in for_slabs:
        copy.wait()
    table_dst = halves(dst[...])
    table_rows = halves(dst[...].T)
    src_cols = dot_left(halves(src[...]), src_hot, NN)
    query = src_cols * rel_cols
    scale, base = coefficient_parts(0, columns, rows, counts, negs)
    coef = coefficients(halves(query), table_rows, scale, base)
    query_grad = dot_split(table_dst, halves(coef), NN)
    src_grad = dot_left(halves(query_grad * rel_cols), src_hot, NT)
    for_state.wait()
    table, state = row_step(src[...], src_state[...], src_grad)
    top, rest = top_out.shape[0], features - top_out.shape[0]
    top_out[...] = table[0:top, :]
    bottom_out[0:rest, :] = table[top:, :]
    bottom_out[rest:, :] = jnp.broadcast_to(state, (bottom_out.shape[0] - rest, columns))
    query_out[...] = query
    coef_out[...] = coef
    product_out[...] = query_grad * src_cols


def first_back_kernel(
    dst, dst_state, query, coef, product, rel, rows, rels, counts, negs,
    spare_state, table_out, state_out, rel_first_out, rel_cols_out, scale_out, base_out, spare_out,
):
    grad = dot_split(halves(query[...]), halves(coef[...]), NT)
    table_out[...], state_out[...] = row_step(dst[...], dst_state[...], grad)
    rel_first_out[...] = dot_right(
        hot_relations(0, rels, rel.shape[0]), halves(product[...]), NT
    )
    rel_cols_out[...] = dot_left(halves(rel[...]), hot_relations(1, rels, rel.shape[0]), TN)
    scale_out[...], base_out[...] = coefficient_parts(1, dst.shape[1], rows, counts, negs)
    spare_out[...] = spare_state[...]


def second_gather_kernel(top, bottom, rel_cols, rows, src_cols_out, high_out, low_out):
    half, features = top.shape[0], rel_cols.shape[0]
    src_hot = as_bf16(onehot(rows[1, 0:1, :], top.shape[1]))
    for low, high, values in ((0, half, top[...]), (half, features, bottom[0 : features - half, :])):
        src_cols = dot_left(halves(values), src_hot, NN)
        src_cols_out[low:high, :] = src_cols
    high_out[...], low_out[...] = halves(src_cols_out[...] * rel_cols[...])


def second_front_kernel(
    spare, src_cols, high, low, rel_cols, scale, base, rels, rel_first, state,
    coef_out, scaled_out, rel_out, state_out,
):
    rel_hot = hot_relations(1, rels, rel_first.shape[0])
    coef = coefficients((high[...], low[...]), halves(spare[...].T), scale[...], base[...])
    query_grad = dot_split(halves(spare[...]), halves(coef), NN)
    pack(rel_out, rel_first[...] + dot_right(rel_hot, halves(query_grad * src_cols[...]), NT))
    state_out[...] = state[...]
    coef_out[...] = coef
    scaled_out[...] = query_grad * rel_cols[...]


def second_back_kernel(
    top, bottom, spare, spare_state, rows, high, low, coef, scaled,
    src_out, src_acc, spare_out, spare_acc,
):
    rest = spare.shape[0] - top.shape[0]
    src_hot = as_bf16(onehot(rows[1, 0:1, :], spare.shape[1]))
    src_grad = dot_left(halves(scaled[...]), src_hot, NT)
    moved = jnp.concatenate([top[...], bottom[0:rest, :]], axis=0)
    src_out[...], src_acc[...] = row_step(moved, bottom[rest : rest + 1, :], src_grad)
    spare_grad = dot_split((high[...], low[...]), halves(coef[...]), NT)
    spare_out[...], spare_acc[...] = row_step(spare[...], spare_state[...], spare_grad)


def add_kernel(left, right, out):
    out[...] = left[...] + right[...]


def relation_kernel(rel, rel_state, *refs):
    terms, (rel_out, state_out) = refs[:-2], refs[-2:]
    total = unpack(tree_sum([term[...] for term in terms]), *rel.shape)
    state = rel_state[...] + total * total
    state_out[...] = state
    rel_out[...] = rel[...] - REL_RATE * total / jnp.sqrt(state)


def call(kernel, in_specs, outs, flops, args, scratch=()):
    shapes = [a if isinstance(a, jax.ShapeDtypeStruct) else jax.ShapeDtypeStruct(a, F32) for a in outs]
    return pl.pallas_call(
        kernel,
        in_specs=in_specs,
        out_specs=[VMEM] * len(outs),
        out_shape=shapes,
        scratch_shapes=list(scratch),
        compiler_params=pltpu.CompilerParams(vmem_limit_bytes=40 * 1024 * 1024),
        cost_estimate=pl.CostEstimate(
            flops=flops, bytes_accessed=sum(a.size * 4 for a in args), transcendentals=0
        ),
    )(*args)


def per_device(
    src_table,
    src_state,
    dst_table,
    dst_state,
    spare_table,
    spare_state,
    relations,
    rel_state,
    edge_rows,
    edge_rel,
    counts,
    negatives,
):
    features, rows = src_table.shape
    edges = edge_rows.shape[2]
    rels = relations.shape[1]
    work = 2 * features * rows * edges
    rel = relations.T
    live = counts.T
    spare_in = swapped(spare_table, "dst", 0)
    operands = [
        src_table, src_state.reshape(1, rows), dst_table, rel, edge_rows, edge_rel, live, negatives,
    ]
    half = features // 16 * 8
    top, bottom, query, coef, product = call(
        first_front_kernel,
        [HBM] * 8,
        [
            (half, rows), (features - half + 8, rows), (features, edges), (rows, edges),
            (features, edges),
        ],
        400 * work,
        [pltpu.with_memory_space_constraint(a, pltpu.HBM) for a in operands],
        [pltpu.VMEM(a.shape, a.dtype) for a in operands]
        + [pltpu.SemaphoreType.DMA((len(operands) + 2,))],
    )
    top, bottom = passed_along((top, bottom), "src", 1)
    dst_next, dst_acc, rel_first, rel_cols, scale, base, spare_acc = call(
        first_back_kernel,
        [VMEM] * 11,
        [
            (features, rows), (1, rows), (rels, features), (features, edges), (rows, edges),
            (rows, edges), (1, rows),
        ],
        3 * work,
        [
            dst_table, dst_state.reshape(1, rows), query, coef, product,
            rel, edge_rows, edge_rel, live, negatives, spare_state.reshape(1, rows),
        ],
    )
    spare_acc_in = swapped(spare_acc, "dst", 0)
    src_cols, high, low = call(
        second_gather_kernel,
        [VMEM] * 4,
        [(features, edges)] + [jax.ShapeDtypeStruct((features, edges), BF16)] * 2,
        2 * work,
        [top, bottom, rel_cols, edge_rows],
    )
    coef, scaled, rel_both, spare_acc_in = call(
        second_front_kernel,
        [VMEM] * 10,
        [(rows, edges), (features, edges), packed_shape(rels, features), (1, rows)],
        10 * work,
        [
            spare_in, src_cols, high, low, rel_cols, scale, base, edge_rel, rel_first,
            spare_acc_in,
        ],
    )
    src_out, src_state_out, spare_out, spare_state_out = call(
        second_back_kernel,
        [VMEM] * 9,
        [(features, rows), (1, rows), (features, rows), (1, rows)],
        5 * work,
        [top, bottom, spare_in, spare_acc_in, edge_rows, high, low, coef, scaled],
    )
    terms = exchanged_terms(rel_both)
    relations_out, rel_state_out = call(
        relation_kernel,
        [VMEM] * (2 + len(terms)),
        [(rels, features), (rels, features)],
        rels * features,
        [rel, rel_state.T, *terms],
    )
    return (
        src_out,
        src_state_out.reshape(rows),
        dst_next,
        dst_acc.reshape(rows),
        spare_out,
        spare_state_out.reshape(rows),
        relations_out.T,
        rel_state_out.T,
    )


def solution(mesh):
    in_specs = (
        P(None, ("src", "dst")),
        P(("src", "dst")),
        P(None, ("src", "dst")),
        P(("src", "dst")),
        P(None, ("src", "dst")),
        P(("src", "dst")),
        P(),
        P(),
        P(None, None, ("src", "dst")),
        P(None, ("src", "dst")),
        P(None, ("src", "dst")),
        P(None, ("src", "dst")),
    )
    out_specs = (
        P(None, ("src", "dst")),
        P(("src", "dst")),
        P(None, ("src", "dst")),
        P(("src", "dst")),
        P(None, ("src", "dst")),
        P(("src", "dst")),
        P(),
        P(),
    )
    return jax.shard_map(
        per_device, mesh=mesh, in_specs=in_specs, out_specs=out_specs, check_vma=False
    )
```

```python
import functools

import jax
import jax.numpy as jnp
from jax import lax
from jax.experimental import pallas as pl
from jax.experimental.pallas import tpu as pltpu
from jax.sharding import PartitionSpec as P

ROW_RATE = 0.25
REL_RATE = 0.5
NEG_WEIGHT = 0.0625
F32 = jnp.float32
BF16 = jnp.bfloat16
NN = (((1,), (0,)), ((), ()))
NT = (((1,), (1,)), ((), ()))
TN = (((0,), (0,)), ((), ()))
VMEM = pl.BlockSpec(memory_space=pltpu.VMEM)
HBM = pl.BlockSpec(memory_space=pltpu.HBM)


def swapped(array, axis, stride):
    return lax.ppermute(array, axis, [(i, i ^ 1 << stride) for i in range(lax.axis_size(axis))])


def passed_along(array, axis, by):
    count = lax.axis_size(axis)
    return lax.ppermute(array, axis, [(i, (i + by) % count) for i in range(count)])


def sent(array, flips):
    n_src, n_dst = lax.axis_size("src"), lax.axis_size("dst")
    pairs = []
    for u in range(n_src):
        for w in range(n_dst):
            src_flip, dst_flip = flips[u % 2]
            pairs.append((u * n_dst + w, (u ^ src_flip) * n_dst + (w ^ dst_flip)))
    return lax.ppermute(array, ("src", "dst"), pairs)


def core_swapped(array):
    return sent(array, ((1, 0), (1, 0)))


def digits(count, unit):
    steps = []
    while count > 1:
        radix = 4 if count % 4 == 0 else 2
        steps.append((radix, unit))
        count, unit = count // radix, unit * radix
    return steps


def exchanged_terms(array, of_chip):
    steps = [(0, r, u) for r, u in digits(lax.axis_size("src") // 2, 2)]
    steps += [(1, r, u) for r, u in digits(lax.axis_size("dst"), 1)]
    terms = None
    for axis, radix, unit in steps:

        def flip(k):
            return (0, k * unit) if axis else (k * unit, 0)

        if terms is None:
            one = sent(array, (flip(1), flip(1)))
            array = of_chip(array, core_swapped(array))
            if radix == 4:
                two = sent(array, (flip(2), flip(2)))
                three = sent(array, (flip(3), flip(3)))
                (late,) = call(add_kernel, [VMEM] * 2, [array.shape], 10**9, [two, three])
                terms = ((array, one + core_swapped(one)), (late,))
            else:
                terms = ((array,), (one + core_swapped(one),))
            continue
        array = tree_sum([tree_sum(pair) for pair in terms])
        if radix == 4:
            odd = sent(array, (flip(1), flip(3)))
            two = sent(array, (flip(2), flip(2)))
            terms = ((array, two), (odd, core_swapped(odd)))
        else:
            terms = ((array,), (sent(array, (flip(1), flip(1))),))
    return [term for pair in terms for term in pair]


def tree_sum(terms):
    terms = list(terms)
    while len(terms) > 1:
        terms = [a + b for a, b in zip(terms[::2], terms[1::2])]
    return terms[0]


def packed_shape(rels, features):
    whole, rest = divmod(features, 128)
    assert rest * rels <= 8 * 128 and rels % 8 == 0
    return (whole * rels + (8 if rest else 0), 128)


def pack(out, values):
    rels, features = values.shape
    whole, rest = divmod(features, 128)
    for k in range(whole):
        out[k * rels : (k + 1) * rels, :] = values[:, k * 128 : (k + 1) * 128]
    if rest:
        tail = [values[8 * k : 8 * (k + 1), whole * 128 :] for k in range(rels // 8)]
        tail.append(jnp.zeros((8, 128 - rest * len(tail)), F32))
        out[whole * rels :, :] = jnp.concatenate(tail, axis=1)


def unpack(packed, rels, features):
    whole, rest = divmod(features, 128)
    parts = [packed[k * rels : (k + 1) * rels, :] for k in range(whole)]
    if rest:
        tail = packed[whole * rels :, :]
        tails = [tail[:, k * rest : (k + 1) * rest] for k in range(rels // 8)]
        parts.append(jnp.concatenate(tails, axis=0))
    return jnp.concatenate(parts, axis=1)


def halves(x):
    high = x.astype(BF16)
    return high, (x - high.astype(F32)).astype(BF16)


def dot(a, b, dims):
    return lax.dot_general(a, b, dims, preferred_element_type=F32)


def stacked(parts, dims, side):
    return jnp.concatenate(parts, axis=dims[0][side][0])


def dot_split(a, b, dims):
    if a[0].shape[dims[0][0][0]] % 128:
        return dot(a[0], b[0], dims) + dot(a[0], b[1], dims) + dot(a[1], b[0], dims)
    left = stacked((a[0], a[0], a[1]), dims, 0)
    return dot(left, stacked((b[0], b[1], b[0]), dims, 1), dims)


def dot_left(a, b, dims):
    if a[0].shape[dims[0][0][0]] % 128:
        return dot(a[0], b, dims) + dot(a[1], b, dims)
    return dot(stacked(a, dims, 0), stacked((b, b), dims, 1), dims)


def dot_right(a, b, dims):
    if b[0].shape[dims[0][1][0]] % 128:
        return dot(a, b[0], dims) + dot(a, b[1], dims)
    return dot(stacked((a, a), dims, 0), stacked(b, dims, 1), dims)


def onehot(index, length):
    return index == lax.broadcasted_iota(jnp.int32, (length, index.shape[1]), 0)


def as_bf16(mask):
    return jnp.where(mask, 1.0, 0.0).astype(BF16)


def negative_weight(negatives, rows, edges):
    ones = jnp.ones((negatives.shape[1], edges), BF16)
    return NEG_WEIGHT * dot(as_bf16(onehot(negatives, rows)), ones, NN)


def coefficient_parts(round_id, columns, edge_rows, counts, negatives):
    edges = edge_rows.shape[2]
    weight = negative_weight(negatives[round_id : round_id + 1, :], columns, edges)
    valid = lax.broadcasted_iota(jnp.int32, (1, edges), 1) < counts[:, round_id : round_id + 1]
    hit = jnp.where(onehot(edge_rows[round_id, 1:2, :], columns), 1.0, 0.0)
    scale = jnp.where(valid, 0.5 * (weight + hit), 0.0)
    return scale, scale - jnp.where(valid, hit, 0.0)


def coefficients(query, table_rows, scale, base):
    return scale * jnp.tanh(0.5 * dot_split(table_rows, query, NN)) + base


def row_step(table, state, gradient):
    new_state = state + jnp.sum(gradient * gradient, axis=0, keepdims=True) * (1.0 / table.shape[0])
    return table - gradient * (ROW_RATE / jnp.sqrt(new_state)), new_state


def hot_relations(round_id, edge_rel, rels):
    return as_bf16(onehot(edge_rel[round_id : round_id + 1, :], rels))


def core_of_chip():
    return lax.rem(lax.axis_index("src"), 2)


def first_front_kernel(core, *refs):
    given, refs = (refs[:3], refs[3:]) if core == 0 else ((), refs)

    @pl.when(core_of_chip() == core)
    def _():
        first_front(*refs)

    if given:

        @pl.when(core_of_chip() != core)
        def _():
            for value, out in zip(given, refs[-12:-9]):
                out[...] = value[...]


def first_front(
    src_hbm, state_hbm, dst_hbm, rel_hbm, rows_hbm, rels_hbm, counts_hbm, negs_hbm, *refs
):
    *moved_outs, query_out, coef_out, product_out = refs[:-9]
    src, src_state, dst, rel, rows, rels, counts, negs, sems = refs[-9:]
    features, columns = src.shape
    small = [
        (rows_hbm, rows), (rels_hbm, rels), (rel_hbm, rel), (counts_hbm, counts), (negs_hbm, negs),
    ]
    slabs = [(dst_hbm, dst), (src_hbm, src)]
    pairs = small + slabs + [(state_hbm, src_state)]
    copies = [pltpu.make_async_copy(a, b, sems.at[i]) for i, (a, b) in enumerate(pairs)]
    for copy in copies:
        copy.start()
    for_dst, for_src, for_state = copies[len(small) :]
    for copy in copies[: len(small)]:
        copy.wait()
    src_hot = as_bf16(onehot(rows[0, 0:1, :], columns))
    rel_cols = dot_left(halves(rel[...]), hot_relations(0, rels, rel.shape[0]), TN)
    for_dst.wait()
    for_src.wait()
    table_dst = halves(dst[...])
    table_rows = halves(dst[...].T)
    src_cols = dot_left(halves(src[...]), src_hot, NN)
    query = src_cols * rel_cols
    scale, base = coefficient_parts(0, columns, rows, counts, negs)
    coef = coefficients(halves(query), table_rows, scale, base)
    query_grad = dot_split(table_dst, halves(coef), NN)
    src_grad = dot_left(halves(query_grad * rel_cols), src_hot, NT)
    for_state.wait()
    table, state = row_step(src[...], src_state[...], src_grad)
    moved = jnp.concatenate([table, jnp.broadcast_to(state, (24, columns))], axis=0)
    low = 0
    for out in moved_outs:
        out[...] = moved[low : low + out.shape[0], :]
        low += out.shape[0]
    query_out[...] = query
    coef_out[...] = coef
    product_out[...] = query_grad * src_cols


def between_kernel(
    dst, dst_state, query, coef, product, rel, rows, rels, counts, negs, spare_state,
    table_out, state_out, rel_first_out, rel_cols_out, scale_out, base_out, spare_out,
):
    grad = dot_split(halves(query[...]), halves(coef[...]), NT)
    table_out[...], state_out[...] = row_step(dst[...], dst_state[...], grad)
    rel_first_out[...] = dot_right(
        hot_relations(0, rels, rel.shape[0]), halves(product[...]), NT
    )
    rel_cols_out[...] = dot_left(halves(rel[...]), hot_relations(1, rels, rel.shape[0]), TN)
    columns = scale_out.shape[0]
    scale_out[...], base_out[...] = coefficient_parts(1, columns, rows, counts, negs)
    spare_out[...] = jnp.broadcast_to(spare_state[...], spare_out.shape)


def second_gather_kernel(count, *refs):
    across, within = refs[:count], refs[count:-6]
    rel_cols, rows, moved_out, src_cols_out, high_out, low_out = refs[-6:]
    moved = jnp.where(
        core_of_chip() == 0,
        jnp.concatenate([part[...] for part in across], axis=0)[0 : moved_out.shape[0], :],
        jnp.concatenate([part[...] for part in within], axis=0)[0 : moved_out.shape[0], :],
    )
    features, columns = src_cols_out.shape[0], moved.shape[1]
    src_hot = as_bf16(onehot(rows[1, 0:1, :], columns))
    src_cols = dot_left(halves(moved[0:features, :]), src_hot, NN)
    high_out[...], low_out[...] = halves(src_cols * rel_cols[...])
    src_cols_out[...] = src_cols
    moved_out[...] = moved


def second_front_kernel(
    spare, src_cols, high, low, rel_cols, scale, base, rels, rel_first,
    coef_out, scaled_out, rel_out,
):
    rel_hot = hot_relations(1, rels, rel_first.shape[0])
    coef = coefficients((high[...], low[...]), halves(spare[...].T), scale[...], base[...])
    query_grad = dot_split(halves(spare[...]), halves(coef), NN)
    pack(rel_out, rel_first[...] + dot_right(rel_hot, halves(query_grad * src_cols[...]), NT))
    coef_out[...] = coef
    scaled_out[...] = query_grad * rel_cols[...]


def second_back_kernel(
    moved, spare, spare_state, rows, high, low, coef, scaled,
    src_out, src_acc, spare_out, spare_acc,
):
    features = spare.shape[0]
    src_hot = as_bf16(onehot(rows[1, 0:1, :], spare.shape[1]))
    src_grad = dot_left(halves(scaled[...]), src_hot, NT)
    src_out[...], src_acc[...] = row_step(
        moved[0:features, :], moved[features : features + 1, :], src_grad
    )
    spare_grad = dot_split((high[...], low[...]), halves(coef[...]), NT)
    spare_out[...], spare_acc[...] = row_step(spare[...], spare_state[...], spare_grad)


def chip_kernel(own, other, state, out, state_out):
    out[...] = own[...] + other[...]
    state_out[...] = state[0:1, :]


def add_kernel(left, right, out):
    out[...] = left[...] + right[...]


def relation_kernel(rel, rel_state, *refs):
    terms, (rel_out, state_out) = refs[:-2], refs[-2:]
    total = unpack(tree_sum([term[...] for term in terms]), *rel.shape)
    state = rel_state[...] + total * total
    state_out[...] = state
    rel_out[...] = rel[...] - REL_RATE * total / jnp.sqrt(state)


def call(kernel, in_specs, outs, flops, args, scratch=()):
    shapes = [a if isinstance(a, jax.ShapeDtypeStruct) else jax.ShapeDtypeStruct(a, F32) for a in outs]
    return pl.pallas_call(
        kernel,
        in_specs=in_specs,
        out_specs=[VMEM] * len(outs),
        out_shape=shapes,
        scratch_shapes=list(scratch),
        compiler_params=pltpu.CompilerParams(vmem_limit_bytes=40 * 1024 * 1024),
        cost_estimate=pl.CostEstimate(
            flops=flops, bytes_accessed=sum(a.size * 4 for a in args), transcendentals=0
        ),
    )(*args)


def cut(length, parts):
    step = -(-length // (8 * parts)) * 8
    return [min(step, length - low) for low in range(0, length, step)]


def per_device(
    src_table,
    src_state,
    dst_table,
    dst_state,
    spare_table,
    spare_state,
    relations,
    rel_state,
    edge_rows,
    edge_rel,
    counts,
    negatives,
):
    features, rows = src_table.shape
    edges = edge_rows.shape[2]
    rels = relations.shape[1]
    work = 2 * features * rows * edges
    rel = relations.T
    live = counts.T
    spare_in = swapped(spare_table, "dst", 0)
    operands = [
        src_table, src_state.reshape(1, rows), dst_table, rel, edge_rows, edge_rel, live, negatives,
    ]
    hbm = [pltpu.with_memory_space_constraint(a, pltpu.HBM) for a in operands]

    def first_on(core, pieces, cost, given=()):
        return call(
            functools.partial(first_front_kernel, core),
            [VMEM] * len(given) + [HBM] * 8,
            [(size, rows) for size in pieces] + [(features, edges), (rows, edges), (features, edges)],
            cost,
            [*given, *hbm],
            [pltpu.VMEM(a.shape, a.dtype) for a in operands]
            + [pltpu.SemaphoreType.DMA((len(operands),))],
        )

    *across, query, coef, product = first_on(1, cut(features + 24, 2), 400 * work)
    across = passed_along(tuple(across), "src", 1)
    *within, query, coef_first, product = first_on(
        0, cut(features + 8, 2), 1 * work, (query, coef, product)
    )
    within = tuple(core_swapped(part) for part in within)
    dst_next, dst_acc, rel_first, rel_cols, scale, base, spare_acc = call(
        between_kernel,
        [VMEM] * 11,
        [(features, rows), (1, rows), (rels, features), (features, edges), (rows, edges), (rows, edges), (40, rows)],
        work,
        [
            dst_table, dst_state.reshape(1, rows), query, coef_first, product,
            rel, edge_rows, edge_rel, live, negatives, spare_state.reshape(1, rows),
        ],
    )
    spare_acc_in = swapped(spare_acc, "dst", 0)
    moved, src_cols, high, low = call(
        functools.partial(second_gather_kernel, len(across)),
        [VMEM] * (len(across) + len(within) + 2),
        [(features + 8, rows), (features, edges)] + [jax.ShapeDtypeStruct((features, edges), BF16)] * 2,
        2 * work,
        [*across, *within, rel_cols, edge_rows],
    )
    coef, scaled, rel_both = call(
        second_front_kernel,
        [VMEM] * 9,
        [(rows, edges), (features, edges), packed_shape(rels, features)],
        10 * work,
        [
            spare_in, src_cols, high, low, rel_cols, scale, base, edge_rel, rel_first,
        ],
    )
    arrived_state = []

    def of_chip(own, other):
        total, state = call(
            chip_kernel, [VMEM] * 3, [own.shape, (1, rows)], 0, [own, other, spare_acc_in]
        )
        arrived_state.append(state)
        return total

    terms = exchanged_terms(rel_both, of_chip)
    (arrived,) = arrived_state
    src_out, src_state_out, spare_out, spare_state_out = call(
        second_back_kernel,
        [VMEM] * 8,
        [(features, rows), (1, rows), (features, rows), (1, rows)],
        5 * work,
        [moved, spare_in, arrived, edge_rows, high, low, coef, scaled],
    )
    relations_out, rel_state_out = call(
        relation_kernel,
        [VMEM] * (2 + len(terms)),
        [(rels, features), (rels, features)],
        rels * features,
        [rel, rel_state.T, *terms],
    )
    return (
        src_out,
        src_state_out.reshape(rows),
        dst_next,
        dst_acc.reshape(rows),
        spare_out,
        spare_state_out.reshape(rows),
        relations_out.T,
        rel_state_out.T,
    )


def solution(mesh):
    in_specs = (
        P(None, ("src", "dst")),
        P(("src", "dst")),
        P(None, ("src", "dst")),
        P(("src", "dst")),
        P(None, ("src", "dst")),
        P(("src", "dst")),
        P(),
        P(),
        P(None, None, ("src", "dst")),
        P(None, ("src", "dst")),
        P(None, ("src", "dst")),
        P(None, ("src", "dst")),
    )
    out_specs = (
        P(None, ("src", "dst")),
        P(("src", "dst")),
        P(None, ("src", "dst")),
        P(("src", "dst")),
        P(None, ("src", "dst")),
        P(("src", "dst")),
        P(),
        P(),
    )
    return jax.shard_map(
        per_device, mesh=mesh, in_specs=in_specs, out_specs=out_specs, check_vma=False
    )
```

```python
import functools

import jax
import jax.numpy as jnp
from jax import lax
from jax.experimental import pallas as pl
from jax.experimental.pallas import tpu as pltpu
from jax.sharding import PartitionSpec as P

ROW_RATE = 0.25
REL_RATE = 0.5
NEG_WEIGHT = 0.0625
F32 = jnp.float32
BF16 = jnp.bfloat16
NN = (((1,), (0,)), ((), ()))
NT = (((1,), (1,)), ((), ()))
TN = (((0,), (0,)), ((), ()))
VMEM = pl.BlockSpec(memory_space=pltpu.VMEM)
HBM = pl.BlockSpec(memory_space=pltpu.HBM)


def swapped(array, axis, stride):
    return lax.ppermute(array, axis, [(i, i ^ 1 << stride) for i in range(lax.axis_size(axis))])


def passed_along(array, axis, by):
    count = lax.axis_size(axis)
    return lax.ppermute(array, axis, [(i, (i + by) % count) for i in range(count)])


def sent(array, flips):
    n_src, n_dst = lax.axis_size("src"), lax.axis_size("dst")
    pairs = []
    for u in range(n_src):
        for w in range(n_dst):
            src_flip, dst_flip = flips[u % 2]
            pairs.append((u * n_dst + w, (u ^ src_flip) * n_dst + (w ^ dst_flip)))
    return lax.ppermute(array, ("src", "dst"), pairs)


def core_swapped(array):
    return sent(array, ((1, 0), (1, 0)))


def digits(count, unit):
    steps = []
    while count > 1:
        radix = 4 if count % 4 == 0 else 2
        steps.append((radix, unit))
        count, unit = count // radix, unit * radix
    return steps


def exchanged_terms(array, of_chip):
    steps = [(0, r, u) for r, u in digits(lax.axis_size("src") // 2, 2)]
    steps += [(1, r, u) for r, u in digits(lax.axis_size("dst"), 1)]
    terms = None
    for axis, radix, unit in steps:

        def flip(k):
            return (0, k * unit) if axis else (k * unit, 0)

        if terms is None:
            one = sent(array, (flip(1), flip(1)))
            array = of_chip(array, core_swapped(array))
            if radix == 4:
                two = sent(array, (flip(2), flip(2)))
                three = sent(array, (flip(3), flip(3)))
                (late,) = call(add_kernel, [VMEM] * 2, [array.shape], 10**9, [two, three])
                terms = ((array, one + core_swapped(one)), (late,))
            else:
                terms = ((array,), (one + core_swapped(one),))
            continue
        array = tree_sum([tree_sum(pair) for pair in terms])
        if radix == 4:
            odd = sent(array, (flip(1), flip(3)))
            two = sent(array, (flip(2), flip(2)))
            terms = ((array, two), (odd, core_swapped(odd)))
        else:
            terms = ((array,), (sent(array, (flip(1), flip(1))),))
    return [term for pair in terms for term in pair]


def tree_sum(terms):
    terms = list(terms)
    while len(terms) > 1:
        terms = [a + b for a, b in zip(terms[::2], terms[1::2])]
    return terms[0]


def packed_shape(rels, features):
    whole, rest = divmod(features, 128)
    assert rest * rels <= 8 * 128 and rels % 8 == 0
    return (whole * rels + (8 if rest else 0), 128)


def pack(out, values):
    rels, features = values.shape
    whole, rest = divmod(features, 128)
    for k in range(whole):
        out[k * rels : (k + 1) * rels, :] = values[:, k * 128 : (k + 1) * 128]
    if rest:
        tail = [values[8 * k : 8 * (k + 1), whole * 128 :] for k in range(rels // 8)]
        tail.append(jnp.zeros((8, 128 - rest * len(tail)), F32))
        out[whole * rels :, :] = jnp.concatenate(tail, axis=1)


def unpack(packed, rels, features):
    whole, rest = divmod(features, 128)
    parts = [packed[k * rels : (k + 1) * rels, :] for k in range(whole)]
    if rest:
        tail = packed[whole * rels :, :]
        tails = [tail[:, k * rest : (k + 1) * rest] for k in range(rels // 8)]
        parts.append(jnp.concatenate(tails, axis=0))
    return jnp.concatenate(parts, axis=1)


def halves(x):
    high = x.astype(BF16)
    return high, (x - high.astype(F32)).astype(BF16)


def dot(a, b, dims):
    return lax.dot_general(a, b, dims, preferred_element_type=F32)


def stacked(parts, dims, side):
    return jnp.concatenate(parts, axis=dims[0][side][0])


def dot_split(a, b, dims):
    if a[0].shape[dims[0][0][0]] % 128:
        return dot(a[0], b[0], dims) + dot(a[0], b[1], dims) + dot(a[1], b[0], dims)
    left = stacked((a[0], a[0], a[1]), dims, 0)
    return dot(left, stacked((b[0], b[1], b[0]), dims, 1), dims)


def dot_left(a, b, dims):
    if a[0].shape[dims[0][0][0]] % 128:
        return dot(a[0], b, dims) + dot(a[1], b, dims)
    return dot(stacked(a, dims, 0), stacked((b, b), dims, 1), dims)


def dot_right(a, b, dims):
    if b[0].shape[dims[0][1][0]] % 128:
        return dot(a, b[0], dims) + dot(a, b[1], dims)
    return dot(stacked((a, a), dims, 0), stacked(b, dims, 1), dims)


def onehot(index, length):
    return index == lax.broadcasted_iota(jnp.int32, (length, index.shape[1]), 0)


def as_bf16(mask):
    return jnp.where(mask, 1.0, 0.0).astype(BF16)


def negative_weight(negatives, rows, edges):
    ones = jnp.ones((negatives.shape[1], edges), BF16)
    return NEG_WEIGHT * dot(as_bf16(onehot(negatives, rows)), ones, NN)


def coefficient_parts(round_id, columns, edge_rows, counts, negatives):
    edges = edge_rows.shape[2]
    weight = negative_weight(negatives[round_id : round_id + 1, :], columns, edges)
    valid = lax.broadcasted_iota(jnp.int32, (1, edges), 1) < counts[:, round_id : round_id + 1]
    hit = jnp.where(onehot(edge_rows[round_id, 1:2, :], columns), 1.0, 0.0)
    scale = jnp.where(valid, 0.5 * (weight + hit), 0.0)
    return scale, scale - jnp.where(valid, hit, 0.0)


def coefficients(query, table_rows, scale, base):
    return scale * jnp.tanh(0.5 * dot_split(table_rows, query, NN)) + base


def row_step(table, state, gradient):
    new_state = state + jnp.sum(gradient * gradient, axis=0, keepdims=True) * (1.0 / table.shape[0])
    return table - gradient * (ROW_RATE / jnp.sqrt(new_state)), new_state


def hot_relations(round_id, edge_rel, rels):
    return as_bf16(onehot(edge_rel[round_id : round_id + 1, :], rels))


def core_of_chip():
    return lax.rem(lax.axis_index("src"), 2)


def first_front_kernel(core, *refs):
    given, refs = (refs[:3], refs[3:]) if core == 0 else ((), refs)

    @pl.when(core_of_chip() == core)
    def _():
        first_front(*refs)

    if given:

        @pl.when(core_of_chip() != core)
        def _():
            for value, out in zip(given, refs[-12:-9]):
                out[...] = value[...]


def first_front(
    src_hbm, state_hbm, dst_hbm, rel_hbm, rows_hbm, rels_hbm, counts_hbm, negs_hbm, *refs
):
    *moved_outs, query_out, coef_out, product_out = refs[:-9]
    src, src_state, dst, rel, rows, rels, counts, negs, sems = refs[-9:]
    features, columns = src.shape
    small = [
        (rows_hbm, rows), (rels_hbm, rels), (rel_hbm, rel), (counts_hbm, counts), (negs_hbm, negs),
    ]
    slabs = [(dst_hbm, dst), (src_hbm, src)]
    pairs = small + slabs + [(state_hbm, src_state)]
    copies = [pltpu.make_async_copy(a, b, sems.at[i]) for i, (a, b) in enumerate(pairs)]
    for copy in copies:
        copy.start()
    for_dst, for_src, for_state = copies[len(small) :]
    for copy in copies[: len(small)]:
        copy.wait()
    src_hot = as_bf16(onehot(rows[0, 0:1, :], columns))
    rel_cols = dot_left(halves(rel[...]), hot_relations(0, rels, rel.shape[0]), TN)
    for_dst.wait()
    for_src.wait()
    table_dst = halves(dst[...])
    table_rows = halves(dst[...].T)
    src_cols = dot_left(halves(src[...]), src_hot, NN)
    query = src_cols * rel_cols
    scale, base = coefficient_parts(0, columns, rows, counts, negs)
    coef = coefficients(halves(query), table_rows, scale, base)
    query_grad = dot_split(table_dst, halves(coef), NN)
    src_grad = dot_left(halves(query_grad * rel_cols), src_hot, NT)
    for_state.wait()
    table, state = row_step(src[...], src_state[...], src_grad)
    moved = jnp.concatenate([table, jnp.broadcast_to(state, (24, columns))], axis=0)
    low = 0
    for out in moved_outs:
        out[...] = moved[low : low + out.shape[0], :]
        low += out.shape[0]
    query_out[...] = query
    coef_out[...] = coef
    product_out[...] = query_grad * src_cols


def between_kernel(
    dst, dst_state, query, coef, product, rel, rows, rels, counts, negs, spare_state,
    table_out, state_out, rel_first_out, rel_cols_out, scale_out, base_out, spare_out,
):
    grad = dot_split(halves(query[...]), halves(coef[...]), NT)
    table_out[...], state_out[...] = row_step(dst[...], dst_state[...], grad)
    rel_first_out[...] = dot_right(
        hot_relations(0, rels, rel.shape[0]), halves(product[...]), NT
    )
    rel_cols_out[...] = dot_left(halves(rel[...]), hot_relations(1, rels, rel.shape[0]), TN)
    columns = scale_out.shape[1]
    scale, base = coefficient_parts(1, columns, rows, counts, negs)
    scale_out[...], base_out[...] = scale.T, base.T
    spare_out[...] = jnp.broadcast_to(spare_state[...], spare_out.shape)


def second_gather_kernel(count, *refs):
    across, within = refs[:count], refs[count:-6]
    rel_cols, rows, moved_out, src_cols_out, high_out, low_out = refs[-6:]
    moved = jnp.where(
        core_of_chip() == 0,
        jnp.concatenate([part[...] for part in across], axis=0)[0 : moved_out.shape[0], :],
        jnp.concatenate([part[...] for part in within], axis=0)[0 : moved_out.shape[0], :],
    )
    features, columns = src_cols_out.shape[0], moved.shape[1]
    src_hot = as_bf16(onehot(rows[1, 0:1, :], columns))
    src_cols = dot_left(halves(moved[0:features, :]), src_hot, NN)
    high_out[...], low_out[...] = halves((src_cols * rel_cols[...]).T)
    src_cols_out[...] = src_cols
    moved_out[...] = moved


def second_front_kernel(
    spare, src_cols, high, low, rel_cols, scale, base, rels, rel_first,
    coef_out, scaled_out, rel_out,
):
    rel_hot = hot_relations(1, rels, rel_first.shape[0])
    table = halves(spare[...])
    coef = coefficients(table, (high[...], low[...]), scale[...], base[...])
    query_grad = dot_split(table, halves(coef), NT)
    pack(rel_out, rel_first[...] + dot_right(rel_hot, halves(query_grad * src_cols[...]), NT))
    coef_out[...] = coef
    scaled_out[...] = query_grad * rel_cols[...]


def second_back_kernel(
    moved, spare, spare_state, rows, high, low, coef, scaled,
    src_out, src_acc, spare_out, spare_acc,
):
    features = spare.shape[0]
    src_hot = as_bf16(onehot(rows[1, 0:1, :], spare.shape[1]))
    src_grad = dot_left(halves(scaled[...]), src_hot, NT)
    src_out[...], src_acc[...] = row_step(
        moved[0:features, :], moved[features : features + 1, :], src_grad
    )
    spare_grad = dot_split((high[...], low[...]), halves(coef[...]), TN)
    spare_out[...], spare_acc[...] = row_step(spare[...], spare_state[...], spare_grad)


def chip_kernel(own, other, state, out, state_out):
    out[...] = own[...] + other[...]
    state_out[...] = state[0:1, :]


def add_kernel(left, right, out):
    out[...] = left[...] + right[...]


def relation_kernel(rel, rel_state, *refs):
    terms, (rel_out, state_out) = refs[:-2], refs[-2:]
    total = unpack(tree_sum([term[...] for term in terms]), *rel.shape)
    state = rel_state[...] + total * total
    state_out[...] = state
    rel_out[...] = rel[...] - REL_RATE * total / jnp.sqrt(state)


def call(kernel, in_specs, outs, flops, args, scratch=()):
    shapes = [a if isinstance(a, jax.ShapeDtypeStruct) else jax.ShapeDtypeStruct(a, F32) for a in outs]
    return pl.pallas_call(
        kernel,
        in_specs=in_specs,
        out_specs=[VMEM] * len(outs),
        out_shape=shapes,
        scratch_shapes=list(scratch),
        compiler_params=pltpu.CompilerParams(vmem_limit_bytes=40 * 1024 * 1024),
        cost_estimate=pl.CostEstimate(
            flops=flops, bytes_accessed=sum(a.size * 4 for a in args), transcendentals=0
        ),
    )(*args)


def cut(length, parts):
    step = -(-length // (8 * parts)) * 8
    return [min(step, length - low) for low in range(0, length, step)]


def per_device(
    src_table,
    src_state,
    dst_table,
    dst_state,
    spare_table,
    spare_state,
    relations,
    rel_state,
    edge_rows,
    edge_rel,
    counts,
    negatives,
):
    features, rows = src_table.shape
    edges = edge_rows.shape[2]
    rels = relations.shape[1]
    work = 2 * features * rows * edges
    rel = relations.T
    live = counts.T
    spare_in = swapped(spare_table, "dst", 0)
    operands = [
        src_table, src_state.reshape(1, rows), dst_table, rel, edge_rows, edge_rel, live, negatives,
    ]
    hbm = [pltpu.with_memory_space_constraint(a, pltpu.HBM) for a in operands]

    def first_on(core, pieces, cost, given=()):
        return call(
            functools.partial(first_front_kernel, core),
            [VMEM] * len(given) + [HBM] * 8,
            [(size, rows) for size in pieces] + [(features, edges), (rows, edges), (features, edges)],
            cost,
            [*given, *hbm],
            [pltpu.VMEM(a.shape, a.dtype) for a in operands]
            + [pltpu.SemaphoreType.DMA((len(operands),))],
        )

    *across, query, coef, product = first_on(1, cut(features + 24, 2), 400 * work)
    across = passed_along(tuple(across), "src", 1)
    *within, query, coef_first, product = first_on(
        0, cut(features + 8, 2), 1 * work, (query, coef, product)
    )
    within = tuple(core_swapped(part) for part in within)
    dst_next, dst_acc, rel_first, rel_cols, scale, base, spare_acc = call(
        between_kernel,
        [VMEM] * 11,
        [(features, rows), (1, rows), (rels, features), (features, edges), (rows, edges), (rows, edges), (40, rows)],
        work,
        [
            dst_table, dst_state.reshape(1, rows), query, coef_first, product,
            rel, edge_rows, edge_rel, live, negatives, spare_state.reshape(1, rows),
        ],
    )
    spare_acc_in = swapped(spare_acc, "dst", 0)
    moved, src_cols, high, low = call(
        functools.partial(second_gather_kernel, len(across)),
        [VMEM] * (len(across) + len(within) + 2),
        [(features + 8, rows), (features, edges)] + [jax.ShapeDtypeStruct((edges, features), BF16)] * 2,
        2 * work,
        [*across, *within, rel_cols, edge_rows],
    )
    coef, scaled, rel_both = call(
        second_front_kernel,
        [VMEM] * 9,
        [(rows, edges), (features, edges), packed_shape(rels, features)],
        10 * work,
        [
            spare_in, src_cols, high, low, rel_cols, scale, base, edge_rel, rel_first,
        ],
    )
    arrived_state = []

    def of_chip(own, other):
        total, state = call(
            chip_kernel, [VMEM] * 3, [own.shape, (1, rows)], 0, [own, other, spare_acc_in]
        )
        arrived_state.append(state)
        return total

    terms = exchanged_terms(rel_both, of_chip)
    (arrived,) = arrived_state
    src_out, src_state_out, spare_out, spare_state_out = call(
        second_back_kernel,
        [VMEM] * 8,
        [(features, rows), (1, rows), (features, rows), (1, rows)],
        5 * work,
        [moved, spare_in, arrived, edge_rows, high, low, coef, scaled],
    )
    relations_out, rel_state_out = call(
        relation_kernel,
        [VMEM] * (2 + len(terms)),
        [(rels, features), (rels, features)],
        rels * features,
        [rel, rel_state.T, *terms],
    )
    return (
        src_out,
        src_state_out.reshape(rows),
        dst_next,
        dst_acc.reshape(rows),
        spare_out,
        spare_state_out.reshape(rows),
        relations_out.T,
        rel_state_out.T,
    )


def solution(mesh):
    in_specs = (
        P(None, ("src", "dst")),
        P(("src", "dst")),
        P(None, ("src", "dst")),
        P(("src", "dst")),
        P(None, ("src", "dst")),
        P(("src", "dst")),
        P(),
        P(),
        P(None, None, ("src", "dst")),
        P(None, ("src", "dst")),
        P(None, ("src", "dst")),
        P(None, ("src", "dst")),
    )
    out_specs = (
        P(None, ("src", "dst")),
        P(("src", "dst")),
        P(None, ("src", "dst")),
        P(("src", "dst")),
        P(None, ("src", "dst")),
        P(("src", "dst")),
        P(),
        P(),
    )
    return jax.shard_map(
        per_device, mesh=mesh, in_specs=in_specs, out_specs=out_specs, check_vma=False
    )
```

```python
import functools

import jax
import jax.numpy as jnp
from jax import lax
from jax.experimental import pallas as pl
from jax.experimental.pallas import tpu as pltpu
from jax.sharding import PartitionSpec as P

ROW_RATE = 0.25
REL_RATE = 0.5
NEG_WEIGHT = 0.0625
F32 = jnp.float32
BF16 = jnp.bfloat16
NN = (((1,), (0,)), ((), ()))
NT = (((1,), (1,)), ((), ()))
TN = (((0,), (0,)), ((), ()))
VMEM = pl.BlockSpec(memory_space=pltpu.VMEM)
HBM = pl.BlockSpec(memory_space=pltpu.HBM)


def swapped(array, axis, stride):
    return lax.ppermute(array, axis, [(i, i ^ 1 << stride) for i in range(lax.axis_size(axis))])


def passed_along(array, axis, by):
    count = lax.axis_size(axis)
    return lax.ppermute(array, axis, [(i, (i + by) % count) for i in range(count)])


def sent(array, flips):
    n_src, n_dst = lax.axis_size("src"), lax.axis_size("dst")
    pairs = []
    for u in range(n_src):
        for w in range(n_dst):
            src_flip, dst_flip = flips[u % 2]
            pairs.append((u * n_dst + w, (u ^ src_flip) * n_dst + (w ^ dst_flip)))
    return lax.ppermute(array, ("src", "dst"), pairs)


def core_swapped(array):
    return sent(array, ((1, 0), (1, 0)))


def digits(count, unit):
    steps = []
    while count > 1:
        radix = 4 if count % 4 == 0 else 2
        steps.append((radix, unit))
        count, unit = count // radix, unit * radix
    return steps


def exchanged_terms(array, of_chip):
    steps = [(0, r, u) for r, u in digits(lax.axis_size("src") // 2, 2)]
    steps += [(1, r, u) for r, u in digits(lax.axis_size("dst"), 1)]
    terms = None
    for axis, radix, unit in steps:

        def flip(k):
            return (0, k * unit) if axis else (k * unit, 0)

        if terms is None:
            one = sent(array, (flip(1), flip(1)))
            array = of_chip(array, core_swapped(array))
            if radix == 4:
                two = sent(array, (flip(2), flip(2)))
                three = sent(array, (flip(3), flip(3)))
                (late,) = call(add_kernel, [VMEM] * 2, [array.shape], 10**9, [two, three])
                terms = ((array, one + core_swapped(one)), (late,))
            else:
                terms = ((array,), (one + core_swapped(one),))
            continue
        array = tree_sum([tree_sum(pair) for pair in terms])
        if radix == 4:
            odd = sent(array, (flip(1), flip(3)))
            two = sent(array, (flip(2), flip(2)))
            terms = ((array, two), (odd, core_swapped(odd)))
        else:
            terms = ((array,), (sent(array, (flip(1), flip(1))),))
    return [term for pair in terms for term in pair]


def tree_sum(terms):
    terms = list(terms)
    while len(terms) > 1:
        terms = [a + b for a, b in zip(terms[::2], terms[1::2])]
    return terms[0]


def packed_shape(rels, features):
    whole, rest = divmod(features, 128)
    assert rest * rels <= 8 * 128 and rels % 8 == 0
    return (whole * rels + (8 if rest else 0), 128)


def pack(out, values):
    rels, features = values.shape
    whole, rest = divmod(features, 128)
    for k in range(whole):
        out[k * rels : (k + 1) * rels, :] = values[:, k * 128 : (k + 1) * 128]
    if rest:
        tail = [values[8 * k : 8 * (k + 1), whole * 128 :] for k in range(rels // 8)]
        tail.append(jnp.zeros((8, 128 - rest * len(tail)), F32))
        out[whole * rels :, :] = jnp.concatenate(tail, axis=1)


def unpack(packed, rels, features):
    whole, rest = divmod(features, 128)
    parts = [packed[k * rels : (k + 1) * rels, :] for k in range(whole)]
    if rest:
        tail = packed[whole * rels :, :]
        tails = [tail[:, k * rest : (k + 1) * rest] for k in range(rels // 8)]
        parts.append(jnp.concatenate(tails, axis=0))
    return jnp.concatenate(parts, axis=1)


def halves(x):
    high = x.astype(BF16)
    return high, (x - high.astype(F32)).astype(BF16)


def dot(a, b, dims):
    return lax.dot_general(a, b, dims, preferred_element_type=F32)


def stacked(parts, dims, side):
    return jnp.concatenate(parts, axis=dims[0][side][0])


def dot_split(a, b, dims):
    if a[0].shape[dims[0][0][0]] % 128:
        return dot(a[0], b[0], dims) + dot(a[0], b[1], dims) + dot(a[1], b[0], dims)
    left = stacked((a[0], a[0], a[1]), dims, 0)
    return dot(left, stacked((b[0], b[1], b[0]), dims, 1), dims)


def dot_left(a, b, dims):
    if a[0].shape[dims[0][0][0]] % 128:
        return dot(a[0], b, dims) + dot(a[1], b, dims)
    return dot(stacked(a, dims, 0), stacked((b, b), dims, 1), dims)


def dot_right(a, b, dims):
    if b[0].shape[dims[0][1][0]] % 128:
        return dot(a, b[0], dims) + dot(a, b[1], dims)
    return dot(stacked((a, a), dims, 0), stacked(b, dims, 1), dims)


def onehot(index, length):
    return index == lax.broadcasted_iota(jnp.int32, (length, index.shape[1]), 0)


def as_bf16(mask):
    return jnp.where(mask, 1.0, 0.0).astype(BF16)


def negative_weight(negatives, rows, edges):
    ones = jnp.ones((negatives.shape[1], edges), BF16)
    return NEG_WEIGHT * dot(as_bf16(onehot(negatives, rows)), ones, NN)


def coefficient_parts(round_id, columns, edge_rows, counts, negatives):
    edges = edge_rows.shape[2]
    weight = negative_weight(negatives[round_id : round_id + 1, :], columns, edges)
    valid = lax.broadcasted_iota(jnp.int32, (1, edges), 1) < counts[:, round_id : round_id + 1]
    hit = jnp.where(onehot(edge_rows[round_id, 1:2, :], columns), 1.0, 0.0)
    scale = jnp.where(valid, 0.5 * (weight + hit), 0.0)
    return scale, scale - jnp.where(valid, hit, 0.0)


def coefficients(query, table_rows, scale, base):
    return scale * jnp.tanh(0.5 * dot_split(table_rows, query, NN)) + base


def row_step(table, state, gradient):
    new_state = state + jnp.sum(gradient * gradient, axis=0, keepdims=True) * (1.0 / table.shape[0])
    return table - gradient * (ROW_RATE * lax.rsqrt(new_state)), new_state


def hot_relations(round_id, edge_rel, rels):
    return as_bf16(onehot(edge_rel[round_id : round_id + 1, :], rels))


def core_of_chip():
    return lax.rem(lax.axis_index("src"), 2)


def first_front_kernel(core, *refs):
    given, refs = (refs[:3], refs[3:]) if core == 0 else ((), refs)

    @pl.when(core_of_chip() == core)
    def _():
        first_front(*refs)

    if given:

        @pl.when(core_of_chip() != core)
        def _():
            for value, out in zip(given, refs[-12:-9]):
                out[...] = value[...]


def first_front(
    src_hbm, state_hbm, dst_hbm, rel_hbm, rows_hbm, rels_hbm, counts_hbm, negs_hbm, *refs
):
    *moved_outs, query_out, coef_out, product_out = refs[:-9]
    src, src_state, dst, rel, rows, rels, counts, negs, sems = refs[-9:]
    features, columns = src.shape
    small = [
        (rows_hbm, rows), (rels_hbm, rels), (rel_hbm, rel), (counts_hbm, counts), (negs_hbm, negs),
    ]
    slabs = [(dst_hbm, dst), (src_hbm, src)]
    pairs = small + slabs + [(state_hbm, src_state)]
    copies = [pltpu.make_async_copy(a, b, sems.at[i]) for i, (a, b) in enumerate(pairs)]
    for copy in copies:
        copy.start()
    for_dst, for_src, for_state = copies[len(small) :]
    for copy in copies[: len(small)]:
        copy.wait()
    src_hot = as_bf16(onehot(rows[0, 0:1, :], columns))
    rel_cols = dot_left(halves(rel[...]), hot_relations(0, rels, rel.shape[0]), TN)
    for_dst.wait()
    for_src.wait()
    table_dst = halves(dst[...])
    table_rows = halves(dst[...].T)
    src_cols = dot_left(halves(src[...]), src_hot, NN)
    query = src_cols * rel_cols
    scale, base = coefficient_parts(0, columns, rows, counts, negs)
    coef = coefficients(halves(query), table_rows, scale, base)
    query_grad = dot_split(table_dst, halves(coef), NN)
    src_grad = dot_left(halves(query_grad * rel_cols), src_hot, NT)
    for_state.wait()
    table, state = row_step(src[...], src_state[...], src_grad)
    moved = jnp.concatenate([table, jnp.broadcast_to(state, (24, columns))], axis=0)
    low = 0
    for out in moved_outs:
        out[...] = moved[low : low + out.shape[0], :]
        low += out.shape[0]
    query_out[...] = query
    coef_out[...] = coef
    product_out[...] = query_grad * src_cols


def between_kernel(
    dst, dst_state, query, coef, product, rel, rows, rels, counts, negs, spare_state,
    table_out, state_out, rel_first_out, rel_cols_out, scale_out, base_out, spare_out,
):
    grad = dot_split(halves(query[...]), halves(coef[...]), NT)
    table_out[...], state_out[...] = row_step(dst[...], dst_state[...], grad)
    rel_first_out[...] = dot_right(
        hot_relations(0, rels, rel.shape[0]), halves(product[...]), NT
    )
    rel_cols_out[...] = dot_left(halves(rel[...]), hot_relations(1, rels, rel.shape[0]), TN)
    columns = scale_out.shape[1]
    scale, base = coefficient_parts(1, columns, rows, counts, negs)
    scale_out[...], base_out[...] = scale.T, base.T
    spare_out[...] = jnp.broadcast_to(spare_state[...], spare_out.shape)


def second_gather_kernel(count, *refs):
    across, within = refs[:count], refs[count:-6]
    rel_cols, rows, moved_out, src_cols_out, high_out, low_out = refs[-6:]
    moved = jnp.where(
        core_of_chip() == 0,
        jnp.concatenate([part[...] for part in across], axis=0)[0 : moved_out.shape[0], :],
        jnp.concatenate([part[...] for part in within], axis=0)[0 : moved_out.shape[0], :],
    )
    features, columns = src_cols_out.shape[0], moved.shape[1]
    src_hot = as_bf16(onehot(rows[1, 0:1, :], columns))
    src_cols = dot_left(halves(moved[0:features, :]), src_hot, NN)
    high_out[...], low_out[...] = halves((src_cols * rel_cols[...]).T)
    src_cols_out[...] = src_cols
    moved_out[...] = moved


def second_front_kernel(
    spare, src_cols, high, low, rel_cols, scale, base, rels, rel_first,
    coef_out, scaled_out, rel_out,
):
    rel_hot = hot_relations(1, rels, rel_first.shape[0])
    table = halves(spare[...])
    coef = coefficients(table, (high[...], low[...]), scale[...], base[...])
    query_grad = dot_split(table, halves(coef), NT)
    pack(rel_out, rel_first[...] + dot_right(rel_hot, halves(query_grad * src_cols[...]), NT))
    coef_out[...] = coef
    scaled_out[...] = query_grad * rel_cols[...]


def second_back_kernel(
    moved, spare, spare_state, rows, high, low, coef, scaled,
    src_out, src_acc, spare_out, spare_acc,
):
    features = spare.shape[0]
    src_hot = as_bf16(onehot(rows[1, 0:1, :], spare.shape[1]))
    src_grad = dot_left(halves(scaled[...]), src_hot, NT)
    src_out[...], src_acc[...] = row_step(
        moved[0:features, :], moved[features : features + 1, :], src_grad
    )
    spare_grad = dot_split((high[...], low[...]), halves(coef[...]), TN)
    spare_out[...], spare_acc[...] = row_step(spare[...], spare_state[...], spare_grad)


def chip_kernel(own, other, state, out, state_out):
    out[...] = own[...] + other[...]
    state_out[...] = state[0:1, :]


def add_kernel(left, right, out):
    out[...] = left[...] + right[...]


def relation_kernel(rel, rel_state, *refs):
    terms, (rel_out, state_out) = refs[:-2], refs[-2:]
    total = unpack(tree_sum([term[...] for term in terms]), *rel.shape)
    state = rel_state[...] + total * total
    state_out[...] = state
    rel_out[...] = rel[...] - REL_RATE * total / jnp.sqrt(state)


def call(kernel, in_specs, outs, flops, args, scratch=()):
    shapes = [a if isinstance(a, jax.ShapeDtypeStruct) else jax.ShapeDtypeStruct(a, F32) for a in outs]
    return pl.pallas_call(
        kernel,
        in_specs=in_specs,
        out_specs=[VMEM] * len(outs),
        out_shape=shapes,
        scratch_shapes=list(scratch),
        compiler_params=pltpu.CompilerParams(vmem_limit_bytes=40 * 1024 * 1024),
        cost_estimate=pl.CostEstimate(
            flops=flops, bytes_accessed=sum(a.size * 4 for a in args), transcendentals=0
        ),
    )(*args)


def cut(length, parts):
    step = -(-length // (8 * parts)) * 8
    return [min(step, length - low) for low in range(0, length, step)]


def per_device(
    src_table,
    src_state,
    dst_table,
    dst_state,
    spare_table,
    spare_state,
    relations,
    rel_state,
    edge_rows,
    edge_rel,
    counts,
    negatives,
):
    features, rows = src_table.shape
    edges = edge_rows.shape[2]
    rels = relations.shape[1]
    work = 2 * features * rows * edges
    rel = relations.T
    live = counts.T
    spare_in = swapped(spare_table, "dst", 0)
    operands = [
        src_table, src_state.reshape(1, rows), dst_table, rel, edge_rows, edge_rel, live, negatives,
    ]
    hbm = [pltpu.with_memory_space_constraint(a, pltpu.HBM) for a in operands]

    def first_on(core, pieces, cost, given=()):
        return call(
            functools.partial(first_front_kernel, core),
            [VMEM] * len(given) + [HBM] * 8,
            [(size, rows) for size in pieces] + [(features, edges), (rows, edges), (features, edges)],
            cost,
            [*given, *hbm],
            [pltpu.VMEM(a.shape, a.dtype) for a in operands]
            + [pltpu.SemaphoreType.DMA((len(operands),))],
        )

    *across, query, coef, product = first_on(1, cut(features + 24, 2), 400 * work)
    across = passed_along(tuple(across), "src", 1)
    *within, query, coef_first, product = first_on(
        0, cut(features + 8, 2), 1 * work, (query, coef, product)
    )
    within = tuple(core_swapped(part) for part in within)
    dst_next, dst_acc, rel_first, rel_cols, scale, base, spare_acc = call(
        between_kernel,
        [VMEM] * 11,
        [(features, rows), (1, rows), (rels, features), (features, edges), (rows, edges), (rows, edges), (40, rows)],
        work,
        [
            dst_table, dst_state.reshape(1, rows), query, coef_first, product,
            rel, edge_rows, edge_rel, live, negatives, spare_state.reshape(1, rows),
        ],
    )
    spare_acc_in = swapped(spare_acc, "dst", 0)
    moved, src_cols, high, low = call(
        functools.partial(second_gather_kernel, len(across)),
        [VMEM] * (len(across) + len(within) + 2),
        [(features + 8, rows), (features, edges)] + [jax.ShapeDtypeStruct((edges, features), BF16)] * 2,
        2 * work,
        [*across, *within, rel_cols, edge_rows],
    )
    coef, scaled, rel_both = call(
        second_front_kernel,
        [VMEM] * 9,
        [(rows, edges), (features, edges), packed_shape(rels, features)],
        10 * work,
        [
            spare_in, src_cols, high, low, rel_cols, scale, base, edge_rel, rel_first,
        ],
    )
    arrived_state = []

    def of_chip(own, other):
        total, state = call(
            chip_kernel, [VMEM] * 3, [own.shape, (1, rows)], 0, [own, other, spare_acc_in]
        )
        arrived_state.append(state)
        return total

    terms = exchanged_terms(rel_both, of_chip)
    (arrived,) = arrived_state
    src_out, src_state_out, spare_out, spare_state_out = call(
        second_back_kernel,
        [VMEM] * 8,
        [(features, rows), (1, rows), (features, rows), (1, rows)],
        5 * work,
        [moved, spare_in, arrived, edge_rows, high, low, coef, scaled],
    )
    relations_out, rel_state_out = call(
        relation_kernel,
        [VMEM] * (2 + len(terms)),
        [(rels, features), (rels, features)],
        rels * features,
        [rel, rel_state.T, *terms],
    )
    return (
        src_out,
        src_state_out.reshape(rows),
        dst_next,
        dst_acc.reshape(rows),
        spare_out,
        spare_state_out.reshape(rows),
        relations_out.T,
        rel_state_out.T,
    )


def solution(mesh):
    in_specs = (
        P(None, ("src", "dst")),
        P(("src", "dst")),
        P(None, ("src", "dst")),
        P(("src", "dst")),
        P(None, ("src", "dst")),
        P(("src", "dst")),
        P(),
        P(),
        P(None, None, ("src", "dst")),
        P(None, ("src", "dst")),
        P(None, ("src", "dst")),
        P(None, ("src", "dst")),
    )
    out_specs = (
        P(None, ("src", "dst")),
        P(("src", "dst")),
        P(None, ("src", "dst")),
        P(("src", "dst")),
        P(None, ("src", "dst")),
        P(("src", "dst")),
        P(),
        P(),
    )
    return jax.shard_map(
        per_device, mesh=mesh, in_specs=in_specs, out_specs=out_specs, check_vma=False
    )
```
